128 devices in a mesh: replica: 16 (over y, z_hi, core), fsdp: 8 (over x, z_lo).
Axes of the slice: x: 4, y: 4, z: 4 (z_hi: 2, z_lo: 2; z = z_hi * 2 + z_lo), core: 2. Of those that a mesh axis runs over, the one named last changes fastest.
Arguments:
- tokens: bfloat16 [16, 3072, 8192], P('replica', 'fsdp'), may hold values from -6 to 6
- queries: bfloat16 [16, 3072, 4096], P('replica', 'fsdp'), may hold values from -250 to 250
- kv_weight: bfloat16 [16, 8192, 1024], P('replica', 'fsdp'), may hold values from -0.06629126 to 0.06629126
- doc_lengths: int32 [16, 8, 6], P('replica', 'fsdp'), may hold values from 1 to 192, 384 in all within a row
- local_params: bfloat16 [16, 1536, 8192], P('replica', 'fsdp'), may hold values from -6 to 6
- base_copy: bfloat16 [1536, 8192], P('fsdp'), may hold values from -6 to 6
- master: float32 [1536, 8192], P('fsdp', 'replica'), may hold values from -6 to 6
- momentum: float32 [1536, 8192], P('fsdp', 'replica'), may hold values from -2 to 2
Outputs:
- attended: bfloat16 [16, 3072, 4096], P('replica', 'fsdp')
- new_master: float32 [1536, 8192], P('fsdp', 'replica')
- new_momentum: float32 [1536, 8192], P('fsdp', 'replica')
- fresh_params: bfloat16 [1536, 8192], P('fsdp')
The draws below stay inside these ranges and needn't reach their ends.
Inputs may be any that keep to these rules, and one draw needn't show every extreme that they name: `doc_lengths`: each device's 6 lengths sum to 384, and the longest is exactly 192.
All inputs are finite; a program needn't handle non-finite values.
Results may differ from the reference program's by a relative error of at most 0.012.
The reference program's roundings to bfloat16 on the way count: a program that leaves them out, or rounds other values in their place, can miss the bound.
Values may be sent and summed in bfloat16 or wider, within the bound.
A program may use at most 192 MiB of HBM per device.

```python
import math
import jax
import jax.numpy as jnp
import numpy as np
from jax import lax

MODEL_WIDTH = 8192
QUERY_HEADS = 32
KEY_VALUE_HEADS = 4
HEAD_SIZE = 128
BLK = 128
SEQS = 6
TOK_DEV = 384
ROWS = 1536
N_REPLICA = 16
N_FSDP = 8


def inner_draws(key):
    feature_matrix = jnp.clip(jax.random.normal(jax.random.fold_in(key, 101), (N_REPLICA, TOK_DEV * N_FSDP, MODEL_WIDTH), jnp.float32), -6.0, 6.0)
    weight_matrix = jnp.clip(jax.random.normal(jax.random.fold_in(key, 102), (N_REPLICA, MODEL_WIDTH, 2 * KEY_VALUE_HEADS * HEAD_SIZE), jnp.float32), -6.0, 6.0) * MODEL_WIDTH ** (-0.5)
    return (feature_matrix, weight_matrix)


def draw_tokens(key, part):
    return inner_draws(key)[0].astype(jnp.bfloat16)


def draw_kv_weight(key, part):
    return inner_draws(key)[1].astype(jnp.bfloat16)


def draw_queries(key, part):
    token_positions = TOK_DEV * N_FSDP
    drawn = jnp.clip(jax.random.normal(jax.random.fold_in(key, 103), (N_REPLICA, token_positions, QUERY_HEADS * HEAD_SIZE), jnp.float32), -6.0, 6.0)
    return drawn.astype(jnp.bfloat16)


def raised(values, own_key, source, target, shards_of, factor):
    def block_of(dim):
        return (jnp.arange(values.shape[dim]) // (values.shape[dim] // shards_of)).reshape((-1,) + (1,) * (values.ndim - 1 - dim))

    one_side = jax.random.permutation(own_key, shards_of)[block_of(target)]
    other_side = (block_of(target) + shards_of // 2) % shards_of
    return jnp.where((block_of(source) == one_side) | (block_of(source) == other_side), factor * values, values)


def block_scale(key, shape, cuts, smallest, top_value):
    level = 1.0
    for position, shards_of in cuts:
        heights = jax.random.uniform(jax.random.fold_in(jax.random.fold_in(key, 6), position), (shards_of,), jnp.float32, smallest / len(cuts), top_value / len(cuts))
        level = level * jnp.repeat(jnp.exp(heights), shape[position] // shards_of).reshape((-1,) + (1,) * (len(shape) - 1 - position))
    return level


def profile(number_of, total, bound, skew):
    loads = [(1 << 20) // math.isqrt(rank ** skew) + 1 for rank in range(2, number_of + 1)]
    spare, counts = total - bound - (number_of - 1), [1] * (number_of - 1)
    while spare > 0:
        candidates = [i for i in range(number_of - 1) if counts[i] < bound]
        mass, budget = sum([loads[i] for i in candidates]), spare
        for i in candidates:
            extra = min(bound - counts[i], max(1, budget * loads[i] // mass), spare)
            counts[i] = counts[i] + extra
            spare = spare - extra
    return np.array([bound] + counts)


def uneven(own_key, amount, total, reach, skew):
    if amount == 2:
        one = jax.random.randint(own_key, (), max(1, total - reach), min(reach, total - 1) + 1)
        return jnp.stack([one, total - one])
    sizes = jnp.asarray(profile(amount, total, reach, skew), jnp.int32)
    pairs = (amount - 1) // 2
    giver, sink = sizes[1:1 + 2 * pairs:2], sizes[2:2 + 2 * pairs:2]
    margin = jnp.minimum(giver - 1, reach - sink)
    passed = jax.random.randint(jax.random.fold_in(own_key, 1), (pairs,), 0, 1 << 20) % (margin + 1)
    sizes = sizes.at[1:1 + 2 * pairs:2].set(giver - passed).at[2:2 + 2 * pairs:2].set(sink + passed)
    return sizes[jax.random.permutation(jax.random.fold_in(own_key, 2), amount)]


def normal_values(own_key, extent, deviation, reach, split=(), held_as=jnp.bfloat16):
    values = deviation * jax.random.normal(own_key, extent, jnp.float32)
    if split:
        values = values * block_scale(own_key, extent, split, -0.22, 0.18)
    return jnp.clip(values, -reach, reach).astype(held_as)


def heavy_noise(rng, shape, spread, reach, split, heavy, held_as=jnp.bfloat16):
    drawn = spread * jax.random.normal(rng, shape, jnp.float32)
    if split:
        drawn = drawn * block_scale(rng, shape, split, -0.22, 0.18)
    return jnp.clip(raised(drawn, jax.random.fold_in(rng, 3), *heavy), -reach, reach).astype(held_as)


def setup_inputs(seed: int = 0) -> dict:
    arg_keys = jax.random.split(jax.random.key(seed), 9)
    return {
        "tokens": draw_tokens(jax.random.fold_in(arg_keys[8], 71), 0),
        "queries": draw_queries(jax.random.fold_in(arg_keys[8], 71), 0),
        "kv_weight": draw_kv_weight(jax.random.fold_in(arg_keys[8], 71), 0),
        "doc_lengths": jax.vmap(lambda own: uneven(own, SEQS, TOK_DEV, TOK_DEV // 2, 2))(jax.random.split(arg_keys[3], N_REPLICA * N_FSDP)).reshape((N_REPLICA, N_FSDP, SEQS)).astype(jnp.int32),
        "local_params": heavy_noise(arg_keys[4], (N_REPLICA, ROWS, MODEL_WIDTH), 1.0, 6.0, ((0, 16), (1, 8)), (0, 2, 16, 2.0)),
        "base_copy": normal_values(arg_keys[5], (ROWS, MODEL_WIDTH), 1.0, 6.0, ((0, 8),)),
        "master": normal_values(arg_keys[6], (ROWS, MODEL_WIDTH), 1.0, 6.0, ((0, 8), (1, 16)), jnp.float32),
        "momentum": normal_values(arg_keys[7], (ROWS, MODEL_WIDTH), 0.3, 2.0, ((0, 8), (1, 16)), jnp.float32),
    }


MOMENTUM_COEF = 0.9
OUTER_RATE = 0.7
QUANT_RANGE = 448.0


def doc_mask(lengths, tok_count):
    doc_ends = jnp.cumsum(lengths)
    places = jnp.arange(tok_count, dtype=jnp.int32)
    doc_index = jnp.sum((places[:, None] >= doc_ends[None, :-1]).astype(jnp.int32), axis=1)
    same_doc = doc_index[:, None] == doc_index[None, :]
    return jnp.logical_and(same_doc, places[None, :] <= places[:, None])


def attend(query_rows, packed, lengths):
    tok_count = query_rows.shape[0]
    head_count = query_rows.shape[1] // HEAD_SIZE
    groups = packed.shape[1] // (2 * HEAD_SIZE)
    key_heads = packed[:, :groups * HEAD_SIZE].reshape(tok_count, groups, HEAD_SIZE).astype(jnp.float32)
    value_heads = packed[:, groups * HEAD_SIZE:].reshape(tok_count, groups, HEAD_SIZE).astype(jnp.float32)
    grouped = query_rows.reshape(tok_count, groups, head_count // groups, HEAD_SIZE).astype(jnp.float32)
    scores = jnp.einsum("tgjd,sgd->gjts", grouped, key_heads) * (HEAD_SIZE ** -0.5)
    allowed = doc_mask(lengths, tok_count)
    scores = jnp.where(allowed[None, None], scores, -1e30)
    highest = jnp.max(scores, axis=-1, keepdims=True)
    expo = jnp.exp(scores - highest)
    attn_weights = (expo / jnp.sum(expo, axis=-1, keepdims=True)).astype(jnp.bfloat16)
    mixed = jnp.einsum("gjts,sgd->tgjd", attn_weights.astype(jnp.float32), value_heads)
    return mixed.reshape(tok_count, head_count * HEAD_SIZE).astype(jnp.bfloat16)


def inner_layer(tokens, queries, kv_weight, doc_lengths):
    def per_replica(replica_args):
        rep_tokens, rep_queries, rep_weight, rep_lengths = replica_args
        rep_tokens = rep_tokens.reshape(N_FSDP, TOK_DEV, MODEL_WIDTH)
        rep_queries = rep_queries.reshape(N_FSDP, TOK_DEV, QUERY_HEADS * HEAD_SIZE)

        def per_block(block_args):
            block_tokens, block_queries, block_lengths = block_args
            packed = jnp.dot(block_tokens, rep_weight, preferred_element_type=jnp.float32).astype(jnp.bfloat16)
            return attend(block_queries, packed, block_lengths)

        result = lax.map(per_block, (rep_tokens, rep_queries, rep_lengths))
        return result.reshape(N_FSDP * TOK_DEV, QUERY_HEADS * HEAD_SIZE)

    return lax.map(per_replica, (tokens, queries, kv_weight, doc_lengths))


def quantize(pseudo_grad):
    row_count = pseudo_grad.shape[0]
    blocked = pseudo_grad.reshape(row_count, MODEL_WIDTH // BLK, BLK)
    scales = ((jnp.max(jnp.abs(blocked), axis=-1) + 1e-6) / QUANT_RANGE).astype(jnp.bfloat16)
    encoded = (blocked / scales.astype(jnp.float32)[..., None]).astype(jnp.bfloat16)
    return encoded, scales


def decode(encoded, scales):
    row_count = encoded.shape[0]
    return (encoded.astype(jnp.float32) * scales.astype(jnp.float32)[..., None]).reshape(row_count, MODEL_WIDTH)


def reference(tokens, queries, kv_weight, doc_lengths, local_params, base_copy, master, momentum):
    attended = inner_layer(tokens, queries, kv_weight, doc_lengths)
    anchor = base_copy.astype(jnp.float32)

    def add_replica(running, local_rows):
        encoded, scales = quantize(anchor - local_rows.astype(jnp.float32))
        return running + decode(encoded, scales), None

    running, _ = lax.scan(add_replica, jnp.zeros(anchor.shape, jnp.float32), local_params)
    averaged = running * (1.0 / N_REPLICA)
    new_momentum = MOMENTUM_COEF * momentum + averaged
    new_master = master - OUTER_RATE * (averaged + MOMENTUM_COEF * new_momentum)
    return attended, new_master, new_momentum, new_master.astype(jnp.bfloat16)
```

```python
import jax
import jax.numpy as jnp
from jax import lax
from jax.experimental import pallas as pl
from jax.experimental.pallas import tpu as pltpu
from jax.sharding import PartitionSpec as P

MESH = pl.DeviceIdType.MESH
HEAD = 128
BLK = 128
MOMENTUM_COEF = 0.9
OUTER_RATE = 0.7
QUANT_RANGE = 448.0

X = 4
Y = 4
FIRST = 448
BF = jnp.bfloat16
F32 = jnp.float32


def kernel(
    tok_h, q_h, w_h, len_s, loc_h, base_h, mast_h, mom_h,
    att_o, nmast_o, nmom_o, fresh_o,
    wbuf, tok, q, att, loc, base, csend, crecv, ysend, yrecv, zsend, zrecv, zown, mast, mom, fbuf, acc, bias,
    kv_send, kv_recv, c_send, c_recv, y_send, y_recv, z_send, z_recv, fz_send, fz_recv, fy_send, fy_recv,
    fc_send, fc_recv, w_sem, in_sem, att_sem, fo_sem, st_sem,
):
    groups = wbuf.shape[0]
    tokens = tok.shape[0]
    shard = w_h.shape[0]
    rows, owned = mast.shape
    pairs = csend.shape[0]
    per_group = q.shape[1] // HEAD // groups
    second = shard - FIRST
    half2 = second // 2

    f = lax.axis_index("fsdp")
    r = lax.axis_index("replica")
    x, z = f // 2, f % 2
    y, zh, core = r // 4, (r // 2) % 2, r % 2

    def place(dx, dz):
        return ((x + dx + X) % X) * 2 + (z + dz) % 2

    def outer(dy, dz, dc):
        return (((y + dy) % Y) * 2 + (zh + dz) % 2) * 2 + (core + dc) % 2

    right = {"fsdp": place(1, 0)}
    left = {"fsdp": place(-1, 0)}
    across = {"fsdp": place(0, 1)}
    twin = {"replica": outer(0, 0, 1)}
    ypeers = [{"replica": outer(d, 0, 0)} for d in range(1, Y)]
    far = {"replica": outer(0, 1, 0)}

    barrier = pltpu.get_barrier_semaphore()
    peers = [right, left, across, twin, far] + ypeers
    for peer in peers:
        pl.semaphore_signal(barrier, inc=1, device_id=peer, device_id_type=MESH)

    def w_copy(g, side):
        return pltpu.make_async_copy(
            w_h.at[:, pl.ds(pl.multiple_of((side * groups + g) * HEAD, HEAD), HEAD)],
            wbuf.at[g, pl.ds(pl.multiple_of(f * shard, 16), shard), pl.ds(side * HEAD, HEAD)],
            w_sem.at[g, side],
        )

    loads = [
        pltpu.make_async_copy(a, b, in_sem.at[i])
        for i, (a, b) in enumerate(
            ((loc_h, loc), (base_h, base), (tok_h, tok), (q_h, q), (mast_h, mast), (mom_h, mom))
        )
    ]
    for g in range(groups):
        for side in range(2):
            w_copy(g, side).start()
    for load in loads:
        load.start()

    kinds = (
        (place(0, 0), FIRST, second, across, place(0, 1)),
        (place(0, 0), 0, FIRST, across, place(0, 1)),
        (place(0, 0), 0, shard, right, place(-1, 0)),
        (place(0, 0), 0, shard, left, place(1, 0)),
        (place(0, 1), FIRST, second, right, place(-1, 1)),
        (place(0, 1), FIRST, second, left, place(1, 1)),
        (place(-1, 0), 0, shard // 2, right, place(2, 0)),
        (place(1, 0), shard // 2, shard // 2, left, place(2, 0)),
        (place(-1, 0), 0, FIRST, across, place(-1, 1)),
        (place(1, 0), 0, FIRST, across, place(1, 1)),
        (place(-1, 1), FIRST, half2, right, place(2, 1)),
        (place(1, 1), FIRST + half2, half2, left, place(2, 1)),
        (place(2, 0), 0, FIRST, across, place(2, 1)),
    )

    def moved(k, g, arriving):
        source, start, count, target, other = kinds[k]
        held = other if arriving else source
        part = wbuf.at[g, pl.ds(pl.multiple_of(held * shard + start, 16), count), :]
        return pltpu.make_async_remote_copy(
            src_ref=part,
            dst_ref=part,
            send_sem=kv_send.at[g, k],
            recv_sem=kv_recv.at[g, k],
            device_id=target,
            device_id_type=MESH,
        )

    def send(g, *which):
        for k in which:
            moved(k, g, False).start()

    def arrived(g, *which):
        for k in which:
            moved(k, g, True).wait_recv()

    def own(g):
        w_copy(g, 0).wait()
        w_copy(g, 1).wait()
        send(g, 0, 2, 3, 1)

    pl.semaphore_wait(barrier, len(peers))
    own(0)
    own(1)

    ends = []
    total = len_s[0]
    for i in range(len_s.shape[0] - 1):
        ends.append(total)
        total = total + len_s[i + 1]
    row_at = lax.broadcasted_iota(jnp.int32, (tokens, 1), 0)
    col_at = lax.broadcasted_iota(jnp.int32, (1, tokens), 1)
    row_doc = jnp.zeros((tokens, 1), jnp.int32)
    col_doc = jnp.zeros((1, tokens), jnp.int32)
    for end in ends:
        row_doc += (row_at >= end).astype(jnp.int32)
        col_doc += (col_at >= end).astype(jnp.int32)
    allowed = jnp.logical_and(row_doc == col_doc, col_at <= row_at)
    bias[...] = jnp.where(allowed, 0.0, -1e30).astype(F32)

    tile = 32

    def decoded(row, col):
        grad = base[pl.ds(row, tile), pl.ds(col, BLK)].astype(F32) - loc[pl.ds(row, tile), pl.ds(col, BLK)].astype(F32)
        top = jnp.max(jnp.abs(grad), axis=1, keepdims=True)
        scale = ((top + 1e-6) / QUANT_RANGE).astype(BF).astype(F32)
        return (grad / scale).astype(BF).astype(F32) * scale

    def over_block(j, side, store):
        first = pl.multiple_of((2 * j + side) * owned, owned)

        def step(t, carry):
            row = pl.multiple_of(t * tile, tile)
            for b in range(owned // BLK):
                store(row, b * BLK, decoded(row, pl.multiple_of(first + b * BLK, BLK)))
            return carry

        lax.fori_loop(0, rows // tile, step, 0)

    def c_copy(j):
        return pltpu.make_async_remote_copy(
            src_ref=csend.at[j], dst_ref=crecv.at[j], send_sem=c_send.at[j], recv_sem=c_recv.at[j],
            device_id=twin, device_id_type=MESH,
        )

    def y_copy(d, arriving):
        part = y if arriving else (y + d) % Y
        return pltpu.make_async_remote_copy(
            src_ref=ysend.at[pl.ds(2 * part, 2)], dst_ref=yrecv.at[d - 1], send_sem=y_send.at[d - 1],
            recv_sem=y_recv.at[d - 1], device_id=ypeers[d - 1], device_id_type=MESH,
        )

    def z_copy():
        return pltpu.make_async_remote_copy(
            src_ref=zsend, dst_ref=zrecv, send_sem=z_send, recv_sem=z_recv, device_id=far, device_id_type=MESH
        )

    def fz_copy(arriving):
        part = fbuf.at[core, 2 * y + (1 - zh if arriving else zh)]
        return pltpu.make_async_remote_copy(
            src_ref=part, dst_ref=part, send_sem=fz_send, recv_sem=fz_recv, device_id=far, device_id_type=MESH
        )

    def fy_copy(d, arriving):
        part = fbuf.at[core, pl.ds(2 * ((y - d + Y) % Y if arriving else y), 2)]
        return pltpu.make_async_remote_copy(
            src_ref=part, dst_ref=part, send_sem=fy_send.at[d - 1], recv_sem=fy_recv.at[d - 1],
            device_id=ypeers[d - 1], device_id_type=MESH,
        )

    def fc_copy(d, arriving):
        at = pl.ds(2 * ((y - d + Y) % Y), 2)
        part = fbuf.at[1 - core, at] if arriving else fbuf.at[core, at]
        return pltpu.make_async_remote_copy(
            src_ref=part, dst_ref=part, send_sem=fc_send.at[d], recv_sem=fc_recv.at[d],
            device_id=twin, device_id_type=MESH,
        )

    def f_out(side, j):
        return pltpu.make_async_copy(
            fbuf.at[side, j],
            fresh_o.at[:, pl.ds(pl.multiple_of((2 * j + side) * owned, owned), owned)],
            fo_sem.at[side, j],
        )

    loads[0].wait()
    loads[1].wait()

    def for_twin(j, carry):
        def store(row, col, value):
            csend[j, pl.ds(row, tile), pl.ds(col, BLK)] = value.astype(BF)

        over_block(j, 1 - core, store)
        c_copy(j).start()
        return carry

    lax.fori_loop(0, pairs, for_twin, 0)

    def with_twin(j, carry):
        c_copy(j).wait_recv()

        def store(row, col, value):
            at = (j, pl.ds(row, tile), pl.ds(col, BLK))
            ysend[at] = (value + crecv[at].astype(F32)).astype(BF)

        over_block(j, core, store)
        return carry

    def sum_y(part, row):
        at = pl.ds(row, tile)
        value = ysend[2 * y + part, at, :].astype(F32)
        for d in range(Y - 1):
            value = value + yrecv[d, part, at, :].astype(F32)
        return value

    def row_tiles(body):
        def step(t, carry):
            body(pl.multiple_of(t * tile, tile))
            return carry

        lax.fori_loop(0, rows // tile, step, 0)

    def att_out(g):
        cols = pl.ds(pl.multiple_of(g * per_group * HEAD, HEAD), per_group * HEAD)
        return pltpu.make_async_copy(att.at[:, cols], att_o.at[:, cols], att_sem.at[g])

    nq = 3
    qrows = tokens // nq

    def compute(g):
        acc[...] = jnp.zeros_like(acc)

        def project(s, carry):
            at = pl.ds(pl.multiple_of(s * shard, shard), shard)
            acc[...] += jnp.dot(tok[:, at], wbuf[g, at, :], preferred_element_type=F32)
            return carry

        lax.fori_loop(0, wbuf.shape[1] // shard, project, 0)
        keys = acc[:, :HEAD].astype(BF)
        values = acc[:, HEAD:].astype(BF)

        def head(j, carry):
            cols = pl.ds(pl.multiple_of((g * per_group + j) * HEAD, HEAD), HEAD)
            for i in range(nq):
                at = pl.ds(i * qrows, qrows)
                seen = (i + 1) * qrows
                scores = lax.dot_general(
                    q[at, cols], keys[:seen], (((1,), (1,)), ((), ())), preferred_element_type=F32
                )
                scores = scores * HEAD**-0.5 + bias[at, :seen]
                expo = jnp.exp(scores - jnp.max(scores, axis=1, keepdims=True))
                weights = (expo / jnp.sum(expo, axis=1, keepdims=True)).astype(BF)
                att[at, cols] = jnp.dot(weights, values[:seen], preferred_element_type=F32).astype(BF)
            return carry

        lax.fori_loop(0, per_group, head, 0)
        att_out(g).start()

    def turn(g, carry):
        @pl.when(g < groups)
        def _():
            arrived(g, 0)
            send(g, 4, 5)
            arrived(g, 2)
            send(g, 6, 8)
            arrived(g, 3)
            send(g, 7, 9)

        @pl.when(g + 2 < groups)
        def _():
            own(g + 2)

        @pl.when(g < groups)
        def _():
            arrived(g, 4)
            send(g, 10)
            arrived(g, 5)
            send(g, 11)
            arrived(g, 6)
            send(g, 12)

        @pl.when(g == 0)
        def _():
            lax.fori_loop(0, pairs, with_twin, 0)
            for d in range(1, Y):
                y_copy(d, False).start()
            loads[2].wait()
            loads[3].wait()
            loads[4].wait()
            loads[5].wait()

        @pl.when(g == 1)
        def _():
            for d in range(1, Y):
                y_copy(d, True).wait_recv()

            def body(row):
                zsend[pl.ds(row, tile), :] = sum_y(1 - zh, row).astype(BF)
                zown[pl.ds(row, tile), :] = sum_y(zh, row)

            row_tiles(body)
            z_copy().start()

        @pl.when(g == 2)
        def _():
            z_copy().wait_recv()

            def body(row):
                at = pl.ds(row, tile)
                averaged = (zown[at, :] + zrecv[at, :].astype(F32)) * (1.0 / 16)
                moved_on = MOMENTUM_COEF * mom[at, :] + averaged
                updated = mast[at, :] - OUTER_RATE * (averaged + MOMENTUM_COEF * moved_on)
                mom[at, :] = moved_on
                mast[at, :] = updated
                fbuf[core, 2 * y + zh, at, :] = updated.astype(BF)

            row_tiles(body)
            fz_copy(False).start()
            pltpu.make_async_copy(mom, nmom_o, st_sem.at[0]).start()
            pltpu.make_async_copy(mast, nmast_o, st_sem.at[1]).start()

        @pl.when(g == 3)
        def _():
            fz_copy(True).wait_recv()
            for d in range(1, Y):
                fy_copy(d, False).start()
            fc_copy(0, False).start()

        @pl.when(g == groups)
        def _():
            for d in range(1, Y):
                fy_copy(d, True).wait_recv()
                fc_copy(d, False).start()

        @pl.when(g > 0)
        def _():
            arrived(g - 1, 1, 7, 8, 9, 10, 11, 12)
            compute(g - 1)

        return carry

    lax.fori_loop(0, groups + 1, turn, 0)

    def out_own(j, carry):
        f_out(core, j).start()
        return carry

    lax.fori_loop(0, pairs, out_own, 0)
    for d in range(Y):
        fc_copy(d, True).wait_recv()

    def out_twin(j, carry):
        f_out(1 - core, j).start()
        return carry

    lax.fori_loop(0, pairs, out_twin, 0)

    def sent(g, carry):
        for k in range(len(kinds)):
            moved(k, g, False).wait_send()
        att_out(g).wait()
        return carry

    lax.fori_loop(0, groups, sent, 0)

    def c_sent(j, carry):
        c_copy(j).wait_send()
        f_out(0, j).wait()
        f_out(1, j).wait()
        return carry

    lax.fori_loop(0, pairs, c_sent, 0)
    for d in range(1, Y):
        y_copy(d, False).wait_send()
        fy_copy(d, False).wait_send()
    for d in range(Y):
        fc_copy(d, False).wait_send()
    z_copy().wait_send()
    fz_copy(False).wait_send()
    pltpu.make_async_copy(mom, nmom_o, st_sem.at[0]).wait()
    pltpu.make_async_copy(mast, nmast_o, st_sem.at[1]).wait()


def shards(tokens, queries, kv_weight, doc_lengths, local_params, base_copy, master, momentum):
    tok_count, width = tokens.shape[1:]
    q_width = queries.shape[2]
    shard, kv_width = kv_weight.shape[1:]
    rows, full = base_copy.shape
    owned = master.shape[1]
    groups = kv_width // (2 * HEAD)
    pairs = full // owned // 2
    hbm = pl.BlockSpec(memory_space=pl.ANY)
    dma = pltpu.SemaphoreType.DMA
    outs = pl.pallas_call(
        kernel,
        out_shape=(
            jax.ShapeDtypeStruct((tok_count, q_width), BF),
            jax.ShapeDtypeStruct((rows, owned), F32),
            jax.ShapeDtypeStruct((rows, owned), F32),
            jax.ShapeDtypeStruct((rows, full), BF),
        ),
        in_specs=[hbm] * 3 + [pl.BlockSpec(memory_space=pltpu.SMEM)] + [hbm] * 4,
        out_specs=(hbm,) * 4,
        scratch_shapes=[
            pltpu.VMEM((groups, width, 2 * HEAD), BF),
            pltpu.VMEM((tok_count, width), BF),
            pltpu.VMEM((tok_count, q_width), BF),
            pltpu.VMEM((tok_count, q_width), BF),
            pltpu.VMEM((rows, full), BF),
            pltpu.VMEM((rows, full), BF),
            pltpu.VMEM((pairs, rows, owned), BF),
            pltpu.VMEM((pairs, rows, owned), BF),
            pltpu.VMEM((pairs, rows, owned), BF),
            pltpu.VMEM((Y - 1, 2, rows, owned), BF),
            pltpu.VMEM((rows, owned), BF),
            pltpu.VMEM((rows, owned), BF),
            pltpu.VMEM((rows, owned), F32),
            pltpu.VMEM((rows, owned), F32),
            pltpu.VMEM((rows, owned), F32),
            pltpu.VMEM((2, pairs, rows, owned), BF),
            pltpu.VMEM((tok_count, 2 * HEAD), F32),
            pltpu.VMEM((tok_count, tok_count), F32),
            dma((groups, 13)),
            dma((groups, 13)),
            dma((pairs,)),
            dma((pairs,)),
            dma((Y - 1,)),
            dma((Y - 1,)),
            dma,
            dma,
            dma,
            dma,
            dma((Y - 1,)),
            dma((Y - 1,)),
            dma((Y,)),
            dma((Y,)),
            dma((groups, 2)),
            dma((6,)),
            dma((groups,)),
            dma((2, pairs)),
            dma((2,)),
        ],
        compiler_params=pltpu.CompilerParams(
            collective_id=0, has_side_effects=True, vmem_limit_bytes=60 * 1024 * 1024
        ),
        cost_estimate=pl.CostEstimate(flops=9 * 10**9, bytes_accessed=3 * 10**7, transcendentals=5 * 10**6),
        name="fused",
    )(
        tokens[0], queries[0], kv_weight[0], doc_lengths[0, 0], local_params[0], base_copy, master, momentum
    )
    attended, new_master, new_momentum, fresh = outs
    return attended[None], new_master, new_momentum, fresh


def solution(mesh):
    return jax.shard_map(
        shards,
        mesh=mesh,
        in_specs=(
            P("replica", "fsdp", None),
            P("replica", "fsdp", None),
            P("replica", "fsdp", None),
            P("replica", "fsdp", None),
            P("replica", "fsdp", None),
            P("fsdp", None),
            P("fsdp", "replica"),
            P("fsdp", "replica"),
        ),
        out_specs=(P("replica", "fsdp", None), P("fsdp", "replica"), P("fsdp", "replica"), P("fsdp", None)),
        check_vma=False,
    )
```

```python
import jax
import jax.numpy as jnp
from jax import lax
from jax.experimental import pallas as pl
from jax.experimental.pallas import tpu as pltpu
from jax.sharding import PartitionSpec as P

MESH = pl.DeviceIdType.MESH
HEAD = 128
BLK = 128
MOMENTUM_COEF = 0.9
OUTER_RATE = 0.7
QUANT_RANGE = 448.0
LOG2E = 1.4426950408889634

X = 4
Y = 4
FIRST = 416
BF = jnp.bfloat16
F32 = jnp.float32


def kernel(
    tok_h, q_h, w_h, len_s, loc_h, base_h, mast_h, mom_h,
    att, mast_o, mom_o, fresh_o,
    wbuf, tok, q, loc, base, csend, crecv, ysend, yhalf, yrecv, zsend, zrecv, zown, mast, mom, fbuf, acc, packed, bias,
    kv_send, kv_recv, c_send, c_recv, y_send, y_recv, z_send, z_recv, fz_send, fz_recv, fy_send, fy_recv,
    fc_send, fc_recv, w_sem, in_sem, fo_sem,
):
    groups = wbuf.shape[0]
    tokens = tok.shape[0]
    shard = w_h.shape[0]
    rows, owned = mast.shape
    pairs = csend.shape[0]
    per_group = q.shape[1] // HEAD // groups
    second = shard - FIRST
    half2 = second // 2

    f = lax.axis_index("fsdp")
    r = lax.axis_index("replica")
    x, z = f // 2, f % 2
    y, zh, core = r // 4, (r // 2) % 2, r % 2

    def place(dx, dz):
        return ((x + dx + X) % X) * 2 + (z + dz) % 2

    def outer(dy, dz, dc):
        return (((y + dy + Y) % Y) * 2 + (zh + dz) % 2) * 2 + (core + dc) % 2

    right = {"fsdp": place(1, 0)}
    left = {"fsdp": place(-1, 0)}
    across = {"fsdp": place(0, 1)}
    twin = {"replica": outer(0, 0, 1)}
    ypeers = [{"replica": outer(d, 0, 0)} for d in (1, -1)]
    far = {"replica": outer(0, 1, 0)}

    barrier = pltpu.get_barrier_semaphore()
    peers = [right, left, across, twin, far] + ypeers
    for peer in peers:
        pl.semaphore_signal(barrier, inc=1, device_id=peer, device_id_type=MESH)

    def w_copy(g, side):
        return pltpu.make_async_copy(
            w_h.at[:, pl.ds(pl.multiple_of((side * groups + g) * HEAD, HEAD), HEAD)],
            wbuf.at[g, pl.ds(pl.multiple_of(f * shard, 16), shard), pl.ds(side * HEAD, HEAD)],
            w_sem.at[g, side],
        )

    loads = [
        pltpu.make_async_copy(a, b, in_sem.at[i])
        for i, (a, b) in enumerate(
            ((loc_h, loc), (base_h, base), (tok_h, tok), (q_h, q), (mast_h, mast), (mom_h, mom))
        )
    ]
    for g in range(groups):
        for side in range(2):
            w_copy(g, side).start()
    for load in loads:
        load.start()

    kinds = (
        (place(0, 0), FIRST, second, across, place(0, 1)),
        (place(0, 0), 0, FIRST, across, place(0, 1)),
        (place(0, 0), 0, shard, right, place(-1, 0)),
        (place(0, 0), 0, shard, left, place(1, 0)),
        (place(0, 1), FIRST, second, right, place(-1, 1)),
        (place(0, 1), FIRST, second, left, place(1, 1)),
        (place(-1, 0), 0, shard // 2, right, place(2, 0)),
        (place(1, 0), shard // 2, shard // 2, left, place(2, 0)),
        (place(-1, 0), 0, FIRST, across, place(-1, 1)),
        (place(1, 0), 0, FIRST, across, place(1, 1)),
        (place(-1, 1), FIRST, half2, right, place(2, 1)),
        (place(1, 1), FIRST + half2, half2, left, place(2, 1)),
        (place(2, 0), 0, FIRST, across, place(2, 1)),
    )

    def moved(k, g, arriving):
        source, start, count, target, other = kinds[k]
        held = other if arriving else source
        part = wbuf.at[g, pl.ds(pl.multiple_of(held * shard + start, 16), count), :]
        return pltpu.make_async_remote_copy(
            src_ref=part,
            dst_ref=part,
            send_sem=kv_send.at[g, k],
            recv_sem=kv_recv.at[g, k],
            device_id=target,
            device_id_type=MESH,
        )

    def send(g, *which):
        for k in which:
            moved(k, g, False).start()

    def arrived(g, *which):
        for k in which:
            moved(k, g, True).wait_recv()

    def own(g):
        w_copy(g, 0).wait()
        w_copy(g, 1).wait()
        send(g, 0, 2, 3, 1)

    pl.semaphore_wait(barrier, len(peers))
    own(0)
    own(1)

    ends = []
    total = len_s[0]
    for i in range(len_s.shape[0] - 1):
        ends.append(total)
        total = total + len_s[i + 1]
    row_at = lax.broadcasted_iota(jnp.int32, (tokens, 1), 0)
    col_at = lax.broadcasted_iota(jnp.int32, (1, tokens), 1)
    row_doc = jnp.zeros((tokens, 1), jnp.int32)
    col_doc = jnp.zeros((1, tokens), jnp.int32)
    for end in ends:
        row_doc += (row_at >= end).astype(jnp.int32)
        col_doc += (col_at >= end).astype(jnp.int32)
    allowed = jnp.logical_and(row_doc == col_doc, col_at <= row_at)
    bias[...] = jnp.where(allowed, 0.0, -1e30).astype(F32)

    tile = 32

    def decoded(row, col):
        grad = base[pl.ds(row, tile), pl.ds(col, BLK)].astype(F32) - loc[pl.ds(row, tile), pl.ds(col, BLK)].astype(F32)
        top = jnp.max(jnp.abs(grad), axis=1, keepdims=True)
        scale = ((top + 1e-6) / QUANT_RANGE).astype(BF).astype(F32)
        return (grad / scale).astype(BF).astype(F32) * scale

    def over_block(j, side, store):
        first = pl.multiple_of((2 * j + side) * owned, owned)

        def step(t, carry):
            row = pl.multiple_of(t * tile, tile)
            for b in range(owned // BLK):
                store(row, b * BLK, decoded(row, pl.multiple_of(first + b * BLK, BLK)))
            return carry

        lax.fori_loop(0, rows // tile, step, 0)

    def c_copy(j):
        return pltpu.make_async_remote_copy(
            src_ref=csend.at[j], dst_ref=crecv.at[j], send_sem=c_send.at[j], recv_sem=c_recv.at[j],
            device_id=twin, device_id_type=MESH,
        )

    def ahead(d):
        return (y + d + Y) % Y

    def y_half(way):
        return pltpu.make_async_remote_copy(
            src_ref=ysend.at[2 * ahead(2) + way], dst_ref=yhalf.at[way], send_sem=y_send.at[way],
            recv_sem=y_recv.at[way], device_id=ypeers[way], device_id_type=MESH,
        )

    def y_pair(way):
        return pltpu.make_async_remote_copy(
            src_ref=ysend.at[pl.ds(2 * ahead(1 - 2 * way), 2)], dst_ref=yrecv.at[way], send_sem=y_send.at[2 + way],
            recv_sem=y_recv.at[2 + way], device_id=ypeers[way], device_id_type=MESH,
        )

    def z_copy():
        return pltpu.make_async_remote_copy(
            src_ref=zsend, dst_ref=zrecv, send_sem=z_send, recv_sem=z_recv, device_id=far, device_id_type=MESH
        )

    def fz_copy(arriving):
        part = fbuf.at[core, 2 * y + (1 - zh if arriving else zh)]
        return pltpu.make_async_remote_copy(
            src_ref=part, dst_ref=part, send_sem=fz_send, recv_sem=fz_recv, device_id=far, device_id_type=MESH
        )

    def f_pair(way, arriving):
        part = fbuf.at[core, pl.ds(2 * (ahead(2 * way - 1) if arriving else y), 2)]
        return pltpu.make_async_remote_copy(
            src_ref=part, dst_ref=part, send_sem=fy_send.at[way], recv_sem=fy_recv.at[way],
            device_id=ypeers[way], device_id_type=MESH,
        )

    def f_half(way, arriving):
        part = fbuf.at[core, 2 * ahead(2 if arriving else 2 * way - 1) + way]
        return pltpu.make_async_remote_copy(
            src_ref=part, dst_ref=part, send_sem=fy_send.at[2 + way], recv_sem=fy_recv.at[2 + way],
            device_id=ypeers[way], device_id_type=MESH,
        )

    def fc_copy(d, arriving):
        at = pl.ds(2 * ahead(d), 2)
        part = fbuf.at[1 - core, at] if arriving else fbuf.at[core, at]
        return pltpu.make_async_remote_copy(
            src_ref=part, dst_ref=part, send_sem=fc_send.at[d + 1], recv_sem=fc_recv.at[d + 1],
            device_id=twin, device_id_type=MESH,
        )

    def f_out(side, j):
        return pltpu.make_async_copy(
            fbuf.at[side, j],
            fresh_o.at[:, pl.ds(pl.multiple_of((2 * j + side) * owned, owned), owned)],
            fo_sem.at[side, j],
        )

    loads[0].wait()
    loads[1].wait()

    def for_twin(j, carry):
        def store(row, col, value):
            csend[j, pl.ds(row, tile), pl.ds(col, BLK)] = value.astype(BF)

        over_block(j, 1 - core, store)
        c_copy(j).start()
        return carry

    lax.fori_loop(0, pairs, for_twin, 0)

    def with_twin(j, carry):
        c_copy(j).wait_recv()

        def store(row, col, value):
            at = (j, pl.ds(row, tile), pl.ds(col, BLK))
            ysend[at] = (value + crecv[at].astype(F32)).astype(BF)

        over_block(j, core, store)
        return carry

    def sum_y(part, row):
        at = pl.ds(row, tile)
        value = ysend[2 * y + part, at, :].astype(F32)
        for way in range(2):
            value = value + yrecv[way, part, at, :].astype(F32)
        return value

    def row_tiles(body):
        def step(t, carry):
            body(pl.multiple_of(t * tile, tile))
            return carry

        lax.fori_loop(0, rows // tile, step, 0)

    nq = 3
    qrows = tokens // nq

    def compute(g):
        def part(held):
            return jnp.dot(
                tok[:, pl.ds(pl.multiple_of(held * shard, shard), shard)],
                wbuf[g, pl.ds(pl.multiple_of(held * shard, shard), shard), :],
                preferred_element_type=F32,
            )

        acc[...] = part(place(0, 0))
        acc[...] += part(place(-1, 0))
        acc[...] += part(place(1, 0))
        for held, which in (
            (place(0, 1), (1,)),
            (place(2, 0), (7,)),
            (place(-1, 1), (8,)),
            (place(1, 1), (9,)),
            (place(2, 1), (10, 11, 12)),
        ):
            arrived(g, *which)
            acc[...] += part(held)
        packed[...] = acc[...].astype(BF)

        heads = [pl.ds(pl.multiple_of((g * per_group + h) * HEAD, HEAD), HEAD) for h in range(per_group)]
        for i in range(nq):
            at = pl.ds(i * qrows, qrows)
            seen = (i + 1) * qrows
            scores = [
                lax.dot_general(
                    q[at, cols], packed[:seen, :HEAD], (((1,), (1,)), ((), ())), preferred_element_type=F32
                )
                * (HEAD**-0.5 * LOG2E)
                + bias[at, :seen]
                for cols in heads
            ]
            highest = [jnp.max(s, axis=1, keepdims=True) for s in scores]
            expo = [jnp.exp2(s - m) for s, m in zip(scores, highest)]
            over = [1.0 / jnp.sum(e, axis=1, keepdims=True) for e in expo]
            for cols, e, o in zip(heads, expo, over):
                weights = (e * o).astype(BF)
                att[at, cols] = jnp.dot(weights, packed[:seen, HEAD:], preferred_element_type=F32).astype(BF)

    def turn(t, carry):
        @pl.when(t == 1)
        def _():
            for way in range(2):
                y_half(way).wait_recv()
                onward = 2 * ahead(1 - 2 * way) + way

                def body(row):
                    at = pl.ds(row, tile)
                    value = ysend[onward, at, :].astype(F32) + yhalf[way, at, :].astype(F32)
                    ysend[onward, at, :] = value.astype(BF)

                row_tiles(body)
                y_pair(way).start()

        @pl.when(t < groups)
        def _():
            arrived(t, 0)
            send(t, 4, 5)
            arrived(t, 2)
            send(t, 6, 8)
            arrived(t, 3)
            send(t, 7, 9)

        @pl.when(jnp.logical_and(t > 0, t <= groups))
        def _():
            arrived(t - 1, 4)
            send(t - 1, 10)
            arrived(t - 1, 5)
            send(t - 1, 11)
            arrived(t - 1, 6)
            send(t - 1, 12)

        @pl.when(t + 2 < groups)
        def _():
            own(t + 2)

        @pl.when(t == 0)
        def _():
            lax.fori_loop(0, pairs, with_twin, 0)
            for way in range(2):
                y_half(way).start()
            for load in loads[2:]:
                load.wait()

        @pl.when(t == 1)
        def _():
            for way in range(2):
                y_pair(way).wait_recv()

            def body(row):
                zsend[pl.ds(row, tile), :] = sum_y(1 - zh, row).astype(BF)
                zown[pl.ds(row, tile), :] = sum_y(zh, row)

            row_tiles(body)
            z_copy().start()

        @pl.when(t == 3)
        def _():
            fz_copy(True).wait_recv()
            for way in range(2):
                f_pair(way, False).start()
            fc_copy(0, False).start()

        @pl.when(t == groups + 1)
        def _():
            def out_own(j, carry):
                f_out(core, j).start()
                return carry

            lax.fori_loop(0, pairs, out_own, 0)
            for d in range(-1, Y - 1):
                fc_copy(d, True).wait_recv()

            def out_twin(j, carry):
                f_out(1 - core, j).start()
                return carry

            lax.fori_loop(0, pairs, out_twin, 0)

        @pl.when(t > 1)
        def _():
            compute(t - 2)

        @pl.when(t == 2)
        def _():
            z_copy().wait_recv()

            def body(row):
                at = pl.ds(row, tile)
                averaged = (zown[at, :] + zrecv[at, :].astype(F32)) * (1.0 / 16)
                moved_on = MOMENTUM_COEF * mom[at, :] + averaged
                updated = mast[at, :] - OUTER_RATE * (averaged + MOMENTUM_COEF * moved_on)
                mom_o[at, :] = moved_on
                mast_o[at, :] = updated
                fbuf[core, 2 * y + zh, at, :] = updated.astype(BF)

            row_tiles(body)
            fz_copy(False).start()

        @pl.when(t == 3)
        def _():
            for way in range(2):
                f_pair(way, True).wait_recv()
                f_half(way, False).start()
                fc_copy(2 * way - 1, False).start()

        @pl.when(t == groups)
        def _():
            for way in range(2):
                f_half(way, True).wait_recv()
            fc_copy(2, False).start()

        return carry

    lax.fori_loop(0, groups + 2, turn, 0)

    def sent(g, carry):
        for k in range(len(kinds)):
            moved(k, g, False).wait_send()
        return carry

    lax.fori_loop(0, groups, sent, 0)

    def c_sent(j, carry):
        c_copy(j).wait_send()
        f_out(0, j).wait()
        f_out(1, j).wait()
        return carry

    lax.fori_loop(0, pairs, c_sent, 0)
    for way in range(2):
        y_half(way).wait_send()
        y_pair(way).wait_send()
        f_pair(way, False).wait_send()
        f_half(way, False).wait_send()
    for d in range(-1, Y - 1):
        fc_copy(d, False).wait_send()
    z_copy().wait_send()
    fz_copy(False).wait_send()


def shards(tokens, queries, kv_weight, doc_lengths, local_params, base_copy, master, momentum):
    tok_count, width = tokens.shape[1:]
    q_width = queries.shape[2]
    shard, kv_width = kv_weight.shape[1:]
    rows, full = base_copy.shape
    owned = master.shape[1]
    groups = kv_width // (2 * HEAD)
    pairs = full // owned // 2
    hbm = pl.BlockSpec(memory_space=pl.ANY)
    dma = pltpu.SemaphoreType.DMA
    outs = pl.pallas_call(
        kernel,
        out_shape=(
            pltpu.VMEM((tok_count, q_width), BF),
            pltpu.VMEM((rows, owned), F32),
            pltpu.VMEM((rows, owned), F32),
            pltpu.VMEM((rows, full), BF),
        ),
        in_specs=[hbm] * 3 + [pl.BlockSpec(memory_space=pltpu.SMEM)] + [hbm] * 4,
        out_specs=(pl.BlockSpec(memory_space=pltpu.VMEM),) * 4,
        scratch_shapes=[
            pltpu.VMEM((groups, width, 2 * HEAD), BF),
            pltpu.VMEM((tok_count, width), BF),
            pltpu.VMEM((tok_count, q_width), BF),
            pltpu.VMEM((rows, full), BF),
            pltpu.VMEM((rows, full), BF),
            pltpu.VMEM((pairs, rows, owned), BF),
            pltpu.VMEM((pairs, rows, owned), BF),
            pltpu.VMEM((pairs, rows, owned), BF),
            pltpu.VMEM((2, rows, owned), BF),
            pltpu.VMEM((2, 2, rows, owned), BF),
            pltpu.VMEM((rows, owned), BF),
            pltpu.VMEM((rows, owned), BF),
            pltpu.VMEM((rows, owned), F32),
            pltpu.VMEM((rows, owned), F32),
            pltpu.VMEM((rows, owned), F32),
            pltpu.VMEM((2, pairs, rows, owned), BF),
            pltpu.VMEM((tok_count, 2 * HEAD), F32),
            pltpu.VMEM((tok_count, 2 * HEAD), BF),
            pltpu.VMEM((tok_count, tok_count), F32),
            dma((groups, 13)),
            dma((groups, 13)),
            dma((pairs,)),
            dma((pairs,)),
            dma((4,)),
            dma((4,)),
            dma,
            dma,
            dma,
            dma,
            dma((4,)),
            dma((4,)),
            dma((Y,)),
            dma((Y,)),
            dma((groups, 2)),
            dma((6,)),
            dma((2, pairs)),
        ],
        compiler_params=pltpu.CompilerParams(
            collective_id=0, has_side_effects=True, vmem_limit_bytes=48 * 1024 * 1024
        ),
        cost_estimate=pl.CostEstimate(flops=9 * 10**9, bytes_accessed=3 * 10**7, transcendentals=5 * 10**6),
        name="fused",
    )(
        tokens[0], queries[0], kv_weight[0], doc_lengths[0, 0], local_params[0], base_copy, master, momentum
    )
    attended, new_master, new_momentum, fresh = outs
    return attended[None], new_master, new_momentum, fresh


def solution(mesh):
    return jax.shard_map(
        shards,
        mesh=mesh,
        in_specs=(
            P("replica", "fsdp", None),
            P("replica", "fsdp", None),
            P("replica", "fsdp", None),
            P("replica", "fsdp", None),
            P("replica", "fsdp", None),
            P("fsdp", None),
            P("fsdp", "replica"),
            P("fsdp", "replica"),
        ),
        out_specs=(P("replica", "fsdp", None), P("fsdp", "replica"), P("fsdp", "replica"), P("fsdp", None)),
        check_vma=False,
    )
```

```python
import jax
import jax.numpy as jnp
from jax import lax
from jax.experimental import pallas as pl
from jax.experimental.pallas import tpu as pltpu
from jax.sharding import PartitionSpec as P

MESH = pl.DeviceIdType.MESH
HEAD = 128
BLK = 128
MOMENTUM_COEF = 0.9
OUTER_RATE = 0.7
QUANT_RANGE = 448.0
LOG2E = 1.4426950408889634

X = 4
Y = 4
LEAD = 2
PARTS = 2
FIRST = 208
BF = jnp.bfloat16
F32 = jnp.float32


def kernel(
    tok_h, q_h, w_h, len_s, loc_h, base_h, mast_h, mom_h,
    att, mast_o, mom_o, fresh_o,
    wbuf, tok, q, loc, base, csend, crecv, ysend, yhalf, yrecv, zsend, zrecv, zown, mast, mom, fbuf, acc, packed, bias,
    kv_send, kv_recv, c_send, c_recv, y_send, y_recv, z_send, z_recv, fz_send, fz_recv, fy_send, fy_recv,
    fc_send, fc_recv, w_sem, in_sem, fo_sem,
):
    chunks = wbuf.shape[0]
    groups = chunks // PARTS
    tokens = tok.shape[0]
    whole = w_h.shape[0]
    shard = whole // PARTS
    rows, owned = mast.shape
    pairs = csend.shape[0]
    per_group = q.shape[1] // HEAD // groups
    second = shard - FIRST
    half2 = (second // 2 + 15) // 16 * 16

    f = lax.axis_index("fsdp")
    r = lax.axis_index("replica")
    x, z = f // 2, f % 2
    y, zh, core = r // 4, (r // 2) % 2, r % 2

    def place(dx, dz):
        return ((x + dx + X) % X) * 2 + (z + dz) % 2

    def outer(dy, dz, dc):
        return (((y + dy + Y) % Y) * 2 + (zh + dz) % 2) * 2 + (core + dc) % 2

    right = {"fsdp": place(1, 0)}
    left = {"fsdp": place(-1, 0)}
    across = {"fsdp": place(0, 1)}
    twin = {"replica": outer(0, 0, 1)}
    ypeers = [{"replica": outer(d, 0, 0)} for d in (1, -1)]
    far = {"replica": outer(0, 1, 0)}

    barrier = pltpu.get_barrier_semaphore()
    peers = [right, left, across, twin, far] + ypeers
    for peer in peers:
        pl.semaphore_signal(barrier, inc=1, device_id=peer, device_id_type=MESH)

    def w_copy(c, side):
        return pltpu.make_async_copy(
            w_h.at[
                pl.ds(pl.multiple_of(c % PARTS * shard, 16), shard),
                pl.ds(pl.multiple_of((side * groups + c // PARTS) * HEAD, HEAD), HEAD),
            ],
            wbuf.at[c, pl.ds(pl.multiple_of(f * shard, 16), shard), pl.ds(side * HEAD, HEAD)],
            w_sem.at[c, side],
        )

    loads = [
        pltpu.make_async_copy(a, b, in_sem.at[i])
        for i, (a, b) in enumerate(
            ((loc_h, loc), (base_h, base), (tok_h, tok), (q_h, q), (mast_h, mast), (mom_h, mom))
        )
    ]
    for c in range(chunks):
        for side in range(2):
            w_copy(c, side).start()
    for load in loads:
        load.start()

    kinds = (
        (place(0, 0), FIRST, second, across, place(0, 1)),
        (place(0, 0), 0, FIRST, across, place(0, 1)),
        (place(0, 0), 0, shard, right, place(-1, 0)),
        (place(0, 0), 0, shard, left, place(1, 0)),
        (place(0, 1), FIRST, second, right, place(-1, 1)),
        (place(0, 1), FIRST, second, left, place(1, 1)),
        (place(-1, 0), 0, shard // 2, right, place(2, 0)),
        (place(1, 0), shard // 2, shard // 2, left, place(2, 0)),
        (place(-1, 0), 0, FIRST, across, place(-1, 1)),
        (place(1, 0), 0, FIRST, across, place(1, 1)),
        (place(-1, 1), FIRST, half2, right, place(2, 1)),
        (place(1, 1), FIRST + half2, second - half2, left, place(2, 1)),
        (place(2, 0), 0, FIRST, across, place(2, 1)),
    )

    def moved(k, g, arriving):
        source, start, count, target, other = kinds[k]
        held = other if arriving else source
        part = wbuf.at[g, pl.ds(pl.multiple_of(held * shard + start, 16), count), :]
        return pltpu.make_async_remote_copy(
            src_ref=part,
            dst_ref=part,
            send_sem=kv_send.at[g, k],
            recv_sem=kv_recv.at[g, k],
            device_id=target,
            device_id_type=MESH,
        )

    def send(g, *which):
        for k in which:
            moved(k, g, False).start()

    def arrived(g, *which):
        for k in which:
            moved(k, g, True).wait_recv()

    def own(g):
        w_copy(g, 0).wait()
        w_copy(g, 1).wait()
        send(g, 0, 2, 3, 1)

    pl.semaphore_wait(barrier, len(peers))
    for c in range(LEAD):
        own(c)

    ends = []
    total = len_s[0]
    for i in range(len_s.shape[0] - 1):
        ends.append(total)
        total = total + len_s[i + 1]
    row_at = lax.broadcasted_iota(jnp.int32, (tokens, 1), 0)
    col_at = lax.broadcasted_iota(jnp.int32, (1, tokens), 1)
    row_doc = jnp.zeros((tokens, 1), jnp.int32)
    col_doc = jnp.zeros((1, tokens), jnp.int32)
    for end in ends:
        row_doc += (row_at >= end).astype(jnp.int32)
        col_doc += (col_at >= end).astype(jnp.int32)
    allowed = jnp.logical_and(row_doc == col_doc, col_at <= row_at)
    bias[...] = jnp.where(allowed, 0.0, -1e30).astype(F32)

    tile = 32

    def decoded(row, col):
        grad = base[pl.ds(row, tile), pl.ds(col, BLK)].astype(F32) - loc[pl.ds(row, tile), pl.ds(col, BLK)].astype(F32)
        top = jnp.max(jnp.abs(grad), axis=1, keepdims=True)
        scale = ((top + 1e-6) / QUANT_RANGE).astype(BF).astype(F32)
        return (grad / scale).astype(BF).astype(F32) * scale

    def over_block(j, side, store):
        first = pl.multiple_of((2 * j + side) * owned, owned)

        def step(t, carry):
            row = pl.multiple_of(t * tile, tile)
            for b in range(owned // BLK):
                store(row, b * BLK, decoded(row, pl.multiple_of(first + b * BLK, BLK)))
            return carry

        lax.fori_loop(0, rows // tile, step, 0)

    def c_copy(j):
        return pltpu.make_async_remote_copy(
            src_ref=csend.at[j], dst_ref=crecv.at[j], send_sem=c_send.at[j], recv_sem=c_recv.at[j],
            device_id=twin, device_id_type=MESH,
        )

    def ahead(d):
        return (y + d + Y) % Y

    def y_half(way):
        return pltpu.make_async_remote_copy(
            src_ref=ysend.at[2 * ahead(2) + way], dst_ref=yhalf.at[way], send_sem=y_send.at[way],
            recv_sem=y_recv.at[way], device_id=ypeers[way], device_id_type=MESH,
        )

    def y_pair(way):
        return pltpu.make_async_remote_copy(
            src_ref=ysend.at[pl.ds(2 * ahead(1 - 2 * way), 2)], dst_ref=yrecv.at[way], send_sem=y_send.at[2 + way],
            recv_sem=y_recv.at[2 + way], device_id=ypeers[way], device_id_type=MESH,
        )

    def z_copy():
        return pltpu.make_async_remote_copy(
            src_ref=zsend, dst_ref=zrecv, send_sem=z_send, recv_sem=z_recv, device_id=far, device_id_type=MESH
        )

    def fz_copy(arriving):
        part = fbuf.at[core, 2 * y + (1 - zh if arriving else zh)]
        return pltpu.make_async_remote_copy(
            src_ref=part, dst_ref=part, send_sem=fz_send, recv_sem=fz_recv, device_id=far, device_id_type=MESH
        )

    def f_pair(way, arriving):
        part = fbuf.at[core, pl.ds(2 * (ahead(2 * way - 1) if arriving else y), 2)]
        return pltpu.make_async_remote_copy(
            src_ref=part, dst_ref=part, send_sem=fy_send.at[way], recv_sem=fy_recv.at[way],
            device_id=ypeers[way], device_id_type=MESH,
        )

    def f_half(way, arriving):
        part = fbuf.at[core, 2 * ahead(2 if arriving else 2 * way - 1) + way]
        return pltpu.make_async_remote_copy(
            src_ref=part, dst_ref=part, send_sem=fy_send.at[2 + way], recv_sem=fy_recv.at[2 + way],
            device_id=ypeers[way], device_id_type=MESH,
        )

    def fc_copy(d, arriving):
        at = pl.ds(2 * ahead(d), 2)
        part = fbuf.at[1 - core, at] if arriving else fbuf.at[core, at]
        return pltpu.make_async_remote_copy(
            src_ref=part, dst_ref=part, send_sem=fc_send.at[d + 1], recv_sem=fc_recv.at[d + 1],
            device_id=twin, device_id_type=MESH,
        )

    def f_out(side, j):
        return pltpu.make_async_copy(
            fbuf.at[side, j],
            fresh_o.at[:, pl.ds(pl.multiple_of((2 * j + side) * owned, owned), owned)],
            fo_sem.at[side, j],
        )

    loads[0].wait()
    loads[1].wait()

    def for_twin(j, carry):
        def store(row, col, value):
            csend[j, pl.ds(row, tile), pl.ds(col, BLK)] = value.astype(BF)

        over_block(j, 1 - core, store)
        c_copy(j).start()
        return carry

    lax.fori_loop(0, pairs, for_twin, 0)

    def with_twin(j, carry):
        c_copy(j).wait_recv()

        def store(row, col, value):
            at = (j, pl.ds(row, tile), pl.ds(col, BLK))
            ysend[at] = (value + crecv[at].astype(F32)).astype(BF)

        over_block(j, core, store)
        return carry

    def sum_y(part, row):
        at = pl.ds(row, tile)
        value = ysend[2 * y + part, at, :].astype(F32)
        for way in range(2):
            value = value + yrecv[way, part, at, :].astype(F32)
        return value

    def row_tiles(body):
        def step(t, carry):
            body(pl.multiple_of(t * tile, tile))
            return carry

        lax.fori_loop(0, rows // tile, step, 0)

    nq = 3
    qrows = tokens // nq

    def compute(c):
        def part(held):
            return jnp.dot(
                tok[:, pl.ds(pl.multiple_of(held * whole + c % PARTS * shard, shard), shard)],
                wbuf[c, pl.ds(pl.multiple_of(held * shard, shard), shard), :],
                preferred_element_type=F32,
            )

        @pl.when(c % PARTS == 0)
        def _():
            acc[...] = jnp.zeros_like(acc)

        acc[...] += part(place(0, 0))
        acc[...] += part(place(-1, 0))
        acc[...] += part(place(1, 0))
        for held, which in (
            (place(0, 1), (1,)),
            (place(2, 0), (7,)),
            (place(-1, 1), (8,)),
            (place(1, 1), (9,)),
            (place(2, 1), (10, 11, 12)),
        ):
            arrived(c, *which)
            acc[...] += part(held)

        @pl.when(c % PARTS == PARTS - 1)
        def _():
            attend(c // PARTS)

    def attend(g):
        packed[...] = acc[...].astype(BF)
        heads = [pl.ds(pl.multiple_of((g * per_group + h) * HEAD, HEAD), HEAD) for h in range(per_group)]
        for i in range(nq):
            at = pl.ds(i * qrows, qrows)
            seen = (i + 1) * qrows
            scores = [
                lax.dot_general(
                    q[at, cols], packed[:seen, :HEAD], (((1,), (1,)), ((), ())), preferred_element_type=F32
                )
                * (HEAD**-0.5 * LOG2E)
                + bias[at, :seen]
                for cols in heads
            ]
            highest = [jnp.max(s, axis=1, keepdims=True) for s in scores]
            expo = [jnp.exp2(s - m) for s, m in zip(scores, highest)]
            over = [1.0 / jnp.sum(e, axis=1, keepdims=True) for e in expo]
            for cols, e, o in zip(heads, expo, over):
                weights = (e * o).astype(BF)
                att[at, cols] = jnp.dot(weights, packed[:seen, HEAD:], preferred_element_type=F32).astype(BF)

    def turn(t, carry):
        @pl.when(t < chunks)
        def _():
            arrived(t, 0)
            send(t, 4, 5)
            arrived(t, 2)
            send(t, 6, 8)
            arrived(t, 3)
            send(t, 7, 9)

        @pl.when(jnp.logical_and(t > 0, t <= chunks))
        def _():
            arrived(t - 1, 4)
            send(t - 1, 10)
            arrived(t - 1, 5)
            send(t - 1, 11)
            arrived(t - 1, 6)
            send(t - 1, 12)

        @pl.when(t + LEAD < chunks)
        def _():
            own(t + LEAD)

        @pl.when(t == 0)
        def _():
            lax.fori_loop(0, pairs, with_twin, 0)
            for way in range(2):
                y_half(way).start()
            for load in loads[2:]:
                load.wait()

        @pl.when(t == 1)
        def _():
            for way in range(2):
                y_half(way).wait_recv()
                onward = 2 * ahead(1 - 2 * way) + way

                def body(row):
                    at = pl.ds(row, tile)
                    value = ysend[onward, at, :].astype(F32) + yhalf[way, at, :].astype(F32)
                    ysend[onward, at, :] = value.astype(BF)

                row_tiles(body)
                y_pair(way).start()

        @pl.when(t == 2)
        def _():
            for way in range(2):
                y_pair(way).wait_recv()

            def body(row):
                zsend[pl.ds(row, tile), :] = sum_y(1 - zh, row).astype(BF)
                zown[pl.ds(row, tile), :] = sum_y(zh, row)

            row_tiles(body)
            z_copy().start()

        @pl.when(t == 4)
        def _():
            z_copy().wait_recv()

            def body(row):
                at = pl.ds(row, tile)
                averaged = (zown[at, :] + zrecv[at, :].astype(F32)) * (1.0 / 16)
                moved_on = MOMENTUM_COEF * mom[at, :] + averaged
                updated = mast[at, :] - OUTER_RATE * (averaged + MOMENTUM_COEF * moved_on)
                mom_o[at, :] = moved_on
                mast_o[at, :] = updated
                fbuf[core, 2 * y + zh, at, :] = updated.astype(BF)

            row_tiles(body)
            fz_copy(False).start()

        @pl.when(t == 6)
        def _():
            fz_copy(True).wait_recv()
            for way in range(2):
                f_pair(way, False).start()
            fc_copy(0, False).start()

        @pl.when(t == 7)
        def _():
            for way in range(2):
                f_pair(way, True).wait_recv()
                f_half(way, False).start()
                fc_copy(2 * way - 1, False).start()

        @pl.when(t == 8)
        def _():
            for way in range(2):
                f_half(way, True).wait_recv()
            fc_copy(2, False).start()

            def out_own(j, carry):
                f_out(core, j).start()
                return carry

            lax.fori_loop(0, pairs, out_own, 0)

        @pl.when(t == chunks + 1)
        def _():
            for d in range(-1, Y - 1):
                fc_copy(d, True).wait_recv()

            def out_twin(j, carry):
                f_out(1 - core, j).start()
                return carry

            lax.fori_loop(0, pairs, out_twin, 0)

        @pl.when(t > 1)
        def _():
            compute(t - 2)

        return carry

    lax.fori_loop(0, chunks + 2, turn, 0)

    def sent(g, carry):
        for k in range(len(kinds)):
            moved(k, g, False).wait_send()
        return carry

    lax.fori_loop(0, chunks, sent, 0)

    def c_sent(j, carry):
        c_copy(j).wait_send()
        f_out(0, j).wait()
        f_out(1, j).wait()
        return carry

    lax.fori_loop(0, pairs, c_sent, 0)
    for way in range(2):
        y_half(way).wait_send()
        y_pair(way).wait_send()
        f_pair(way, False).wait_send()
        f_half(way, False).wait_send()
    for d in range(-1, Y - 1):
        fc_copy(d, False).wait_send()
    z_copy().wait_send()
    fz_copy(False).wait_send()


def write_out(a, b, c, d, a_o, b_o, c_o, d_o, sem):
    copies = [
        pltpu.make_async_copy(src, dst, sem.at[i])
        for i, (src, dst) in enumerate(((a, a_o), (d, d_o), (b, b_o), (c, c_o)))
    ]
    for copy in copies:
        copy.start()
    for copy in copies:
        copy.wait()


def shards(tokens, queries, kv_weight, doc_lengths, local_params, base_copy, master, momentum):
    tok_count, width = tokens.shape[1:]
    q_width = queries.shape[2]
    shard, kv_width = kv_weight.shape[1:]
    rows, full = base_copy.shape
    owned = master.shape[1]
    groups = kv_width // (2 * HEAD)
    pairs = full // owned // 2
    hbm = pl.BlockSpec(memory_space=pl.ANY)
    dma = pltpu.SemaphoreType.DMA
    outs = pl.pallas_call(
        kernel,
        out_shape=(
            pltpu.VMEM((tok_count, q_width), BF),
            pltpu.VMEM((rows, owned), F32),
            pltpu.VMEM((rows, owned), F32),
            pltpu.VMEM((rows, full), BF),
        ),
        in_specs=[hbm] * 3 + [pl.BlockSpec(memory_space=pltpu.SMEM)] + [hbm] * 4,
        out_specs=(pl.BlockSpec(memory_space=pltpu.VMEM),) * 4,
        scratch_shapes=[
            pltpu.VMEM((groups * PARTS, width // PARTS, 2 * HEAD), BF),
            pltpu.VMEM((tok_count, width), BF),
            pltpu.VMEM((tok_count, q_width), BF),
            pltpu.VMEM((rows, full), BF),
            pltpu.VMEM((rows, full), BF),
            pltpu.VMEM((pairs, rows, owned), BF),
            pltpu.VMEM((pairs, rows, owned), BF),
            pltpu.VMEM((pairs, rows, owned), BF),
            pltpu.VMEM((2, rows, owned), BF),
            pltpu.VMEM((2, 2, rows, owned), BF),
            pltpu.VMEM((rows, owned), BF),
            pltpu.VMEM((rows, owned), BF),
            pltpu.VMEM((rows, owned), F32),
            pltpu.VMEM((rows, owned), F32),
            pltpu.VMEM((rows, owned), F32),
            pltpu.VMEM((2, pairs, rows, owned), BF),
            pltpu.VMEM((tok_count, 2 * HEAD), F32),
            pltpu.VMEM((tok_count, 2 * HEAD), BF),
            pltpu.VMEM((tok_count, tok_count), F32),
            dma((groups * PARTS, 13)),
            dma((groups * PARTS, 13)),
            dma((pairs,)),
            dma((pairs,)),
            dma((4,)),
            dma((4,)),
            dma,
            dma,
            dma,
            dma,
            dma((4,)),
            dma((4,)),
            dma((Y,)),
            dma((Y,)),
            dma((groups * PARTS, 2)),
            dma((6,)),
            dma((2, pairs)),
        ],
        compiler_params=pltpu.CompilerParams(
            collective_id=0, has_side_effects=True, vmem_limit_bytes=48 * 1024 * 1024
        ),
        cost_estimate=pl.CostEstimate(flops=9 * 10**9, bytes_accessed=3 * 10**7, transcendentals=5 * 10**6),
        name="fused",
    )(
        tokens[0], queries[0], kv_weight[0], doc_lengths[0, 0], local_params[0], base_copy, master, momentum
    )
    attended, new_master, new_momentum, fresh = pl.pallas_call(
        write_out,
        out_shape=tuple(jax.ShapeDtypeStruct(o.shape, o.dtype) for o in outs),
        in_specs=[pl.BlockSpec(memory_space=pltpu.VMEM)] * 4,
        out_specs=(hbm,) * 4,
        scratch_shapes=[dma((4,))],
        compiler_params=pltpu.CompilerParams(vmem_limit_bytes=2 * 1024 * 1024),
        name="write_out",
    )(*outs)
    return attended[None], new_master, new_momentum, fresh


def solution(mesh):
    return jax.shard_map(
        shards,
        mesh=mesh,
        in_specs=(
            P("replica", "fsdp", None),
            P("replica", "fsdp", None),
            P("replica", "fsdp", None),
            P("replica", "fsdp", None),
            P("replica", "fsdp", None),
            P("fsdp", None),
            P("fsdp", "replica"),
            P("fsdp", "replica"),
        ),
        out_specs=(P("replica", "fsdp", None), P("fsdp", "replica"), P("fsdp", "replica"), P("fsdp", None)),
        check_vma=False,
    )
```

```python
import jax
import jax.numpy as jnp
from jax import lax
from jax.experimental import pallas as pl
from jax.experimental.pallas import tpu as pltpu
from jax.sharding import PartitionSpec as P

MESH = pl.DeviceIdType.MESH
HEAD = 128
BLK = 128
MOMENTUM_COEF = 0.9
OUTER_RATE = 0.7
QUANT_RANGE = 448.0
LOG2E = 1.4426950408889634

X = 4
Y = 4
LEAD = 2
PARTS = 2
BF = jnp.bfloat16
F32 = jnp.float32


def kernel(
    tok_h, q_h, w_h, len_s, loc_h, base_h, mast_h, mom_h,
    att, mast_o, mom_o, fresh_o,
    wbuf, tok, q, loc, base, csend, crecv, ysend, yhalf, yrecv, zsend, zrecv, zown, mast, mom, fbuf, acc, given, gained, theirs, packed, bias,
    kv_send, kv_recv, tok_send, tok_recv, g_send, g_recv, c_send, c_recv, y_send, y_recv, z_send, z_recv, fz_send, fz_recv, fy_send, fy_recv,
    fc_send, fc_recv, w_sem, in_sem, fo_sem,
):
    chunks = wbuf.shape[0]
    groups = chunks // PARTS
    tokens = tok.shape[0]
    whole = w_h.shape[0]
    shard = whole // PARTS
    rows, owned = mast.shape
    pairs = csend.shape[0]
    per_group = q.shape[1] // HEAD // groups
    half = shard // 2
    quarter = shard // 4

    f = lax.axis_index("fsdp")
    r = lax.axis_index("replica")
    x, z = f // 2, f % 2
    y, zh, core = r // 4, (r // 2) % 2, r % 2

    def place(dx, dz):
        return ((x + dx + X) % X) * 2 + (z + dz) % 2

    def outer(dy, dz, dc):
        return (((y + dy + Y) % Y) * 2 + (zh + dz) % 2) * 2 + (core + dc) % 2

    right = {"fsdp": place(1, 0)}
    left = {"fsdp": place(-1, 0)}
    across = {"fsdp": place(0, 1)}
    twin = {"replica": outer(0, 0, 1)}
    ypeers = [{"replica": outer(d, 0, 0)} for d in (1, -1)]
    far = {"replica": outer(0, 1, 0)}

    barrier = pltpu.get_barrier_semaphore()
    peers = [right, left, across, twin, far] + ypeers
    for peer in peers:
        pl.semaphore_signal(barrier, inc=1, device_id=peer, device_id_type=MESH)

    def w_copy(c, side):
        return pltpu.make_async_copy(
            w_h.at[
                pl.ds(pl.multiple_of(c // groups * shard, 16), shard),
                pl.ds(pl.multiple_of((side * groups + c % groups) * HEAD, HEAD), HEAD),
            ],
            wbuf.at[c, pl.ds(pl.multiple_of(f * shard, 16), shard), pl.ds(side * HEAD, HEAD)],
            w_sem.at[c, side],
        )

    loads = [
        pltpu.make_async_copy(a, b, in_sem.at[i])
        for i, (a, b) in enumerate(
            ((loc_h, loc), (base_h, base), (tok_h, tok), (q_h, q), (mast_h, mast), (mom_h, mom))
        )
    ]
    for c in range(chunks):
        for side in range(2):
            w_copy(c, side).start()
    for load in loads:
        load.start()

    kinds = (
        (place(0, 0), half, half, across, place(0, 1)),
        (place(0, 0), 0, shard, right, place(-1, 0)),
        (place(0, 0), 0, shard, left, place(1, 0)),
        (place(0, 1), half, half, right, place(-1, 1)),
        (place(0, 1), half, half, left, place(1, 1)),
        (place(-1, 0), 0, half, right, place(2, 0)),
        (place(1, 0), half, half, left, place(2, 0)),
        (place(-1, 1), half, quarter, right, place(2, 1)),
        (place(1, 1), half + quarter, quarter, left, place(2, 1)),
    )

    def tok_copy(h, xx, arriving):
        cols = pl.ds(pl.multiple_of((xx * 2 + 1 - z) * whole + h * shard, half), half)
        there = theirs.at[:, pl.ds((h * X + xx) * half, half)]
        return pltpu.make_async_remote_copy(
            src_ref=there if arriving else tok.at[:, cols], dst_ref=there, send_sem=tok_send.at[h, xx],
            recv_sem=tok_recv.at[h, xx], device_id=across, device_id_type=MESH,
        )

    def sums_back(g):
        return pltpu.make_async_remote_copy(
            src_ref=given.at[g], dst_ref=gained.at[g], send_sem=g_send.at[g], recv_sem=g_recv.at[g],
            device_id=across, device_id_type=MESH,
        )

    def moved(k, g, arriving):
        source, start, count, target, other = kinds[k]
        held = other if arriving else source
        part = wbuf.at[g, pl.ds(pl.multiple_of(held * shard + start, 16), count), :]
        return pltpu.make_async_remote_copy(
            src_ref=part,
            dst_ref=part,
            send_sem=kv_send.at[g, k],
            recv_sem=kv_recv.at[g, k],
            device_id=target,
            device_id_type=MESH,
        )

    def send(g, *which):
        for k in which:
            moved(k, g, False).start()

    def arrived(g, *which):
        for k in which:
            moved(k, g, True).wait_recv()

    def own(g):
        w_copy(g, 0).wait()
        w_copy(g, 1).wait()
        send(g, 0, 1, 2)

    pl.semaphore_wait(barrier, len(peers))
    for c in range(LEAD):
        own(c)

    loads[2].wait()
    for xx in range(X):
        tok_copy(0, xx, False).start()
    given[...] = jnp.zeros_like(given)
    acc[...] = jnp.zeros_like(acc)

    ends = []
    total = len_s[0]
    for i in range(len_s.shape[0] - 1):
        ends.append(total)
        total = total + len_s[i + 1]
    row_at = lax.broadcasted_iota(jnp.int32, (tokens, 1), 0)
    col_at = lax.broadcasted_iota(jnp.int32, (1, tokens), 1)
    row_doc = jnp.zeros((tokens, 1), jnp.int32)
    col_doc = jnp.zeros((1, tokens), jnp.int32)
    for end in ends:
        row_doc += (row_at >= end).astype(jnp.int32)
        col_doc += (col_at >= end).astype(jnp.int32)
    allowed = jnp.logical_and(row_doc == col_doc, col_at <= row_at)
    bias[...] = jnp.where(allowed, 0.0, -1e30).astype(F32)

    tile = 32

    def decoded(row, col):
        grad = base[pl.ds(row, tile), pl.ds(col, BLK)].astype(F32) - loc[pl.ds(row, tile), pl.ds(col, BLK)].astype(F32)
        top = jnp.max(jnp.abs(grad), axis=1, keepdims=True)
        scale = ((top + 1e-6) / QUANT_RANGE).astype(BF).astype(F32)
        return (grad / scale).astype(BF).astype(F32) * scale

    def over_block(j, side, store):
        first = pl.multiple_of((2 * j + side) * owned, owned)

        def step(t, carry):
            row = pl.multiple_of(t * tile, tile)
            for b in range(owned // BLK):
                store(row, b * BLK, decoded(row, pl.multiple_of(first + b * BLK, BLK)))
            return carry

        lax.fori_loop(0, rows // tile, step, 0)

    def c_copy(j):
        return pltpu.make_async_remote_copy(
            src_ref=csend.at[j], dst_ref=crecv.at[j], send_sem=c_send.at[j], recv_sem=c_recv.at[j],
            device_id=twin, device_id_type=MESH,
        )

    def ahead(d):
        return (y + d + Y) % Y

    def y_half(way):
        return pltpu.make_async_remote_copy(
            src_ref=ysend.at[2 * ahead(2) + way], dst_ref=yhalf.at[way], send_sem=y_send.at[way],
            recv_sem=y_recv.at[way], device_id=ypeers[way], device_id_type=MESH,
        )

    def y_pair(way):
        return pltpu.make_async_remote_copy(
            src_ref=ysend.at[pl.ds(2 * ahead(1 - 2 * way), 2)], dst_ref=yrecv.at[way], send_sem=y_send.at[2 + way],
            recv_sem=y_recv.at[2 + way], device_id=ypeers[way], device_id_type=MESH,
        )

    def z_copy():
        return pltpu.make_async_remote_copy(
            src_ref=zsend, dst_ref=zrecv, send_sem=z_send, recv_sem=z_recv, device_id=far, device_id_type=MESH
        )

    def fz_copy(arriving):
        part = fbuf.at[core, 2 * y + (1 - zh if arriving else zh)]
        return pltpu.make_async_remote_copy(
            src_ref=part, dst_ref=part, send_sem=fz_send, recv_sem=fz_recv, device_id=far, device_id_type=MESH
        )

    def f_pair(way, arriving):
        part = fbuf.at[core, pl.ds(2 * (ahead(2 * way - 1) if arriving else y), 2)]
        return pltpu.make_async_remote_copy(
            src_ref=part, dst_ref=part, send_sem=fy_send.at[way], recv_sem=fy_recv.at[way],
            device_id=ypeers[way], device_id_type=MESH,
        )

    def f_half(way, arriving):
        part = fbuf.at[core, 2 * ahead(2 if arriving else 2 * way - 1) + way]
        return pltpu.make_async_remote_copy(
            src_ref=part, dst_ref=part, send_sem=fy_send.at[2 + way], recv_sem=fy_recv.at[2 + way],
            device_id=ypeers[way], device_id_type=MESH,
        )

    def fc_copy(d, arriving):
        at = pl.ds(2 * ahead(d), 2)
        part = fbuf.at[1 - core, at] if arriving else fbuf.at[core, at]
        return pltpu.make_async_remote_copy(
            src_ref=part, dst_ref=part, send_sem=fc_send.at[d + 1], recv_sem=fc_recv.at[d + 1],
            device_id=twin, device_id_type=MESH,
        )

    def f_out(side, j):
        return pltpu.make_async_copy(
            fbuf.at[side, j],
            fresh_o.at[:, pl.ds(pl.multiple_of((2 * j + side) * owned, owned), owned)],
            fo_sem.at[side, j],
        )

    loads[0].wait()
    loads[1].wait()

    def for_twin(j, carry):
        def store(row, col, value):
            csend[j, pl.ds(row, tile), pl.ds(col, BLK)] = value.astype(BF)

        over_block(j, 1 - core, store)
        c_copy(j).start()
        return carry

    lax.fori_loop(0, pairs, for_twin, 0)

    def with_twin(j, carry):
        c_copy(j).wait_recv()

        def store(row, col, value):
            at = (j, pl.ds(row, tile), pl.ds(col, BLK))
            ysend[at] = (value + crecv[at].astype(F32)).astype(BF)

        over_block(j, core, store)
        return carry

    def sum_y(part, row):
        at = pl.ds(row, tile)
        value = ysend[2 * y + part, at, :].astype(F32)
        for way in range(2):
            value = value + yrecv[way, part, at, :].astype(F32)
        return value

    def row_tiles(body):
        def step(t, carry):
            body(pl.multiple_of(t * tile, tile))
            return carry

        lax.fori_loop(0, rows // tile, step, 0)

    nq = 3
    qrows = tokens // nq

    def product(tokens_of, first, c, row, count):
        return jnp.dot(
            tokens_of[:, pl.ds(pl.multiple_of(first, half), count)],
            wbuf[c, pl.ds(pl.multiple_of(row, half), count), :],
            preferred_element_type=F32,
        )

    def give(c):
        g, h = c % groups, c // groups
        for xx in range(X):
            given[g] += product(theirs, (h * X + xx) * half, c, (xx * 2 + z) * shard, half)

    def compute(c):
        g, h = c % groups, c // groups

        def add(held, start, count):
            acc[g] += product(tok, held * whole + h * shard + start, c, held * shard + start, count)

        add(place(0, 0), 0, shard)
        add(place(-1, 0), 0, shard)
        add(place(1, 0), 0, shard)
        add(place(0, 1), half, half)
        add(place(-1, 1), half, half)
        add(place(1, 1), half, half)
        arrived(c, 6)
        add(place(2, 0), 0, shard)
        arrived(c, 7, 8)
        add(place(2, 1), half, half)

        @pl.when(h == PARTS - 1)
        def _():
            sums_back(g).wait_recv()
            attend(g)

    def attend(g):
        packed[...] = (acc[g] + gained[g]).astype(BF)
        heads = [pl.ds(pl.multiple_of((g * per_group + h) * HEAD, HEAD), HEAD) for h in range(per_group)]
        for i in range(nq):
            at = pl.ds(i * qrows, qrows)
            seen = (i + 1) * qrows
            scores = [
                lax.dot_general(
                    q[at, cols], packed[:seen, :HEAD], (((1,), (1,)), ((), ())), preferred_element_type=F32
                )
                * (HEAD**-0.5 * LOG2E)
                + bias[at, :seen]
                for cols in heads
            ]
            highest = [jnp.max(s, axis=1, keepdims=True) for s in scores]
            expo = [jnp.exp2(s - m) for s, m in zip(scores, highest)]
            over = [1.0 / jnp.sum(e, axis=1, keepdims=True) for e in expo]
            for cols, e, o in zip(heads, expo, over):
                weights = (e * o).astype(BF)
                att[at, cols] = jnp.dot(weights, packed[:seen, HEAD:], preferred_element_type=F32).astype(BF)

    def turn(t, carry):
        @pl.when(t < chunks)
        def _():
            arrived(t, 1)
            send(t, 5)
            arrived(t, 2)
            send(t, 6)

        @pl.when(t + LEAD < chunks)
        def _():
            own(t + LEAD)

        @pl.when(t == 1)
        def _():
            for xx in range(X // 2):
                tok_copy(1, xx, False).start()

        @pl.when(t == 2)
        def _():
            for xx in range(X // 2, X):
                tok_copy(1, xx, False).start()

        @pl.when(t == 1)
        def _():
            for xx in range(X):
                tok_copy(0, xx, True).wait_recv()

        @pl.when(t == groups + 1)
        def _():
            for xx in range(X):
                tok_copy(1, xx, True).wait_recv()

        @pl.when(jnp.logical_and(t > 1, t <= chunks + 1))
        def _():
            arrived(t - 2, 0)
            send(t - 2, 3, 4)

        @pl.when(jnp.logical_and(t > 0, t <= chunks))
        def _():
            arrived(t - 1, 5)
            give(t - 1)

        @pl.when(jnp.logical_and(t > groups, t <= chunks))
        def _():
            sums_back(t - 1 - groups).start()

        @pl.when(jnp.logical_and(t > 2, t <= chunks + 2))
        def _():
            arrived(t - 3, 3)
            send(t - 3, 7)
            arrived(t - 3, 4)
            send(t - 3, 8)

        @pl.when(t == 0)
        def _():
            lax.fori_loop(0, pairs, with_twin, 0)
            for way in range(2):
                y_half(way).start()
            for load in loads[3:]:
                load.wait()

        @pl.when(t == 1)
        def _():
            for way in range(2):
                y_half(way).wait_recv()
                onward = 2 * ahead(1 - 2 * way) + way

                def body(row):
                    at = pl.ds(row, tile)
                    value = ysend[onward, at, :].astype(F32) + yhalf[way, at, :].astype(F32)
                    ysend[onward, at, :] = value.astype(BF)

                row_tiles(body)
                y_pair(way).start()

        @pl.when(t == 2)
        def _():
            for way in range(2):
                y_pair(way).wait_recv()

            def body(row):
                zsend[pl.ds(row, tile), :] = sum_y(1 - zh, row).astype(BF)
                zown[pl.ds(row, tile), :] = sum_y(zh, row)

            row_tiles(body)
            z_copy().start()

        @pl.when(t == 4)
        def _():
            z_copy().wait_recv()

            def body(row):
                at = pl.ds(row, tile)
                averaged = (zown[at, :] + zrecv[at, :].astype(F32)) * (1.0 / 16)
                moved_on = MOMENTUM_COEF * mom[at, :] + averaged
                updated = mast[at, :] - OUTER_RATE * (averaged + MOMENTUM_COEF * moved_on)
                mom_o[at, :] = moved_on
                mast_o[at, :] = updated
                fbuf[core, 2 * y + zh, at, :] = updated.astype(BF)

            row_tiles(body)
            fz_copy(False).start()

        @pl.when(t == 6)
        def _():
            fz_copy(True).wait_recv()
            for way in range(2):
                f_pair(way, False).start()
            fc_copy(0, False).start()

        @pl.when(t == 7)
        def _():
            for way in range(2):
                f_pair(way, True).wait_recv()
                f_half(way, False).start()
                fc_copy(2 * way - 1, False).start()

        @pl.when(t == 8)
        def _():
            for way in range(2):
                f_half(way, True).wait_recv()
            fc_copy(2, False).start()

            def out_own(j, carry):
                f_out(core, j).start()
                return carry

            lax.fori_loop(0, pairs, out_own, 0)

        @pl.when(t == chunks + 2)
        def _():
            for d in range(-1, Y - 1):
                fc_copy(d, True).wait_recv()

            def out_twin(j, carry):
                f_out(1 - core, j).start()
                return carry

            lax.fori_loop(0, pairs, out_twin, 0)

        @pl.when(t > 3)
        def _():
            compute(t - 4)

        return carry

    lax.fori_loop(0, chunks + 4, turn, 0)

    def sent(g, carry):
        for k in range(len(kinds)):
            moved(k, g, False).wait_send()
        return carry

    lax.fori_loop(0, chunks, sent, 0)
    for h in range(PARTS):
        for xx in range(X):
            tok_copy(h, xx, False).wait_send()
    for g in range(groups):
        sums_back(g).wait_send()

    def c_sent(j, carry):
        c_copy(j).wait_send()
        f_out(0, j).wait()
        f_out(1, j).wait()
        return carry

    lax.fori_loop(0, pairs, c_sent, 0)
    for way in range(2):
        y_half(way).wait_send()
        y_pair(way).wait_send()
        f_pair(way, False).wait_send()
        f_half(way, False).wait_send()
    for d in range(-1, Y - 1):
        fc_copy(d, False).wait_send()
    z_copy().wait_send()
    fz_copy(False).wait_send()


def write_out(a, b, c, d, a_o, b_o, c_o, d_o, sem):
    copies = [
        pltpu.make_async_copy(src, dst, sem.at[i])
        for i, (src, dst) in enumerate(((a, a_o), (d, d_o), (b, b_o), (c, c_o)))
    ]
    for copy in copies:
        copy.start()
    for copy in copies:
        copy.wait()


def shards(tokens, queries, kv_weight, doc_lengths, local_params, base_copy, master, momentum):
    tok_count, width = tokens.shape[1:]
    q_width = queries.shape[2]
    shard, kv_width = kv_weight.shape[1:]
    rows, full = base_copy.shape
    owned = master.shape[1]
    groups = kv_width // (2 * HEAD)
    pairs = full // owned // 2
    hbm = pl.BlockSpec(memory_space=pl.ANY)
    dma = pltpu.SemaphoreType.DMA
    outs = pl.pallas_call(
        kernel,
        out_shape=(
            pltpu.VMEM((tok_count, q_width), BF),
            pltpu.VMEM((rows, owned), F32),
            pltpu.VMEM((rows, owned), F32),
            pltpu.VMEM((rows, full), BF),
        ),
        in_specs=[hbm] * 3 + [pl.BlockSpec(memory_space=pltpu.SMEM)] + [hbm] * 4,
        out_specs=(pl.BlockSpec(memory_space=pltpu.VMEM),) * 4,
        scratch_shapes=[
            pltpu.VMEM((groups * PARTS, width // PARTS, 2 * HEAD), BF),
            pltpu.VMEM((tok_count, width), BF),
            pltpu.VMEM((tok_count, q_width), BF),
            pltpu.VMEM((rows, full), BF),
            pltpu.VMEM((rows, full), BF),
            pltpu.VMEM((pairs, rows, owned), BF),
            pltpu.VMEM((pairs, rows, owned), BF),
            pltpu.VMEM((pairs, rows, owned), BF),
            pltpu.VMEM((2, rows, owned), BF),
            pltpu.VMEM((2, 2, rows, owned), BF),
            pltpu.VMEM((rows, owned), BF),
            pltpu.VMEM((rows, owned), BF),
            pltpu.VMEM((rows, owned), F32),
            pltpu.VMEM((rows, owned), F32),
            pltpu.VMEM((rows, owned), F32),
            pltpu.VMEM((2, pairs, rows, owned), BF),
            pltpu.VMEM((groups, tok_count, 2 * HEAD), F32),
            pltpu.VMEM((groups, tok_count, 2 * HEAD), F32),
            pltpu.VMEM((groups, tok_count, 2 * HEAD), F32),
            pltpu.VMEM((tok_count, width // 4), BF),
            pltpu.VMEM((tok_count, 2 * HEAD), BF),
            pltpu.VMEM((tok_count, tok_count), F32),
            dma((groups * PARTS, 9)),
            dma((groups * PARTS, 9)),
            dma((PARTS, X)),
            dma((PARTS, X)),
            dma((groups,)),
            dma((groups,)),
            dma((pairs,)),
            dma((pairs,)),
            dma((4,)),
            dma((4,)),
            dma,
            dma,
            dma,
            dma,
            dma((4,)),
            dma((4,)),
            dma((Y,)),
            dma((Y,)),
            dma((groups * PARTS, 2)),
            dma((6,)),
            dma((2, pairs)),
        ],
        compiler_params=pltpu.CompilerParams(
            collective_id=0, has_side_effects=True, vmem_limit_bytes=51 * 1024 * 1024
        ),
        cost_estimate=pl.CostEstimate(flops=9 * 10**9, bytes_accessed=3 * 10**7, transcendentals=5 * 10**6),
        name="fused",
    )(
        tokens[0], queries[0], kv_weight[0], doc_lengths[0, 0], local_params[0], base_copy, master, momentum
    )
    attended, new_master, new_momentum, fresh = pl.pallas_call(
        write_out,
        out_shape=tuple(jax.ShapeDtypeStruct(o.shape, o.dtype) for o in outs),
        in_specs=[pl.BlockSpec(memory_space=pltpu.VMEM)] * 4,
        out_specs=(hbm,) * 4,
        scratch_shapes=[dma((4,))],
        compiler_params=pltpu.CompilerParams(vmem_limit_bytes=2 * 1024 * 1024),
        name="write_out",
    )(*outs)
    return attended[None], new_master, new_momentum, fresh


def solution(mesh):
    return jax.shard_map(
        shards,
        mesh=mesh,
        in_specs=(
            P("replica", "fsdp", None),
            P("replica", "fsdp", None),
            P("replica", "fsdp", None),
            P("replica", "fsdp", None),
            P("replica", "fsdp", None),
            P("fsdp", None),
            P("fsdp", "replica"),
            P("fsdp", "replica"),
        ),
        out_specs=(P("replica", "fsdp", None), P("fsdp", "replica"), P("fsdp", "replica"), P("fsdp", None)),
        check_vma=False,
    )
```

```python
import jax
import jax.numpy as jnp
from jax import lax
from jax.experimental import pallas as pl
from jax.experimental.pallas import tpu as pltpu
from jax.sharding import PartitionSpec as P

MESH = pl.DeviceIdType.MESH
HEAD = 128
BLK = 128
MOMENTUM_COEF = 0.9
OUTER_RATE = 0.7
QUANT_RANGE = 448.0
LOG2E = 1.4426950408889634

X = 4
Y = 4
LEAD = 2
PARTS = 2
BF = jnp.bfloat16
F32 = jnp.float32


def attend(q, q_first, packed, bias, att, att_first, heads):
    tokens = q.shape[0]
    nq = 3
    qrows = tokens // nq
    from_cols = [pl.ds(pl.multiple_of(q_first + h * HEAD, HEAD), HEAD) for h in range(heads)]
    to_cols = [pl.ds(pl.multiple_of(att_first + h * HEAD, HEAD), HEAD) for h in range(heads)]
    for i in range(nq):
        at = pl.ds(i * qrows, qrows)
        seen = (i + 1) * qrows
        scores = [
            lax.dot_general(q[at, cols], packed[:seen, :HEAD], (((1,), (1,)), ((), ())), preferred_element_type=F32)
            * (HEAD**-0.5 * LOG2E)
            + bias[at, :seen]
            for cols in from_cols
        ]
        highest = [jnp.max(s, axis=1, keepdims=True) for s in scores]
        expo = [jnp.exp2(s - m) for s, m in zip(scores, highest)]
        over = [1.0 / jnp.sum(e, axis=1, keepdims=True) for e in expo]
        for cols, e, o in zip(to_cols, expo, over):
            weights = (e * o).astype(BF)
            att[at, cols] = jnp.dot(weights, packed[:seen, HEAD:], preferred_element_type=F32).astype(BF)


def kernel(
    tok_h, q_h, w_h, len_s, loc_h, base_h, mast_h, mom_h,
    att, mast_o, mom_o, fresh_o, packed, bias,
    wbuf, tok, q, loc, base, csend, crecv, ysend, yhalf, yrecv, zsend, zrecv, zown, mast, mom, fbuf, acc, given, gained, theirs,
    kv_send, kv_recv, tok_send, tok_recv, g_send, g_recv, c_send, c_recv, y_send, y_recv, z_send, z_recv, fz_send, fz_recv, fy_send, fy_recv,
    fc_send, fc_recv, w_sem, in_sem, fo_sem,
):
    chunks = wbuf.shape[0]
    groups = chunks // PARTS
    tokens = tok.shape[0]
    whole = w_h.shape[0]
    shard = whole // PARTS
    rows, owned = mast.shape
    pairs = csend.shape[0]
    per_group = q.shape[1] // HEAD // groups
    half = shard // 2
    quarter = shard // 4

    f = lax.axis_index("fsdp")
    r = lax.axis_index("replica")
    x, z = f // 2, f % 2
    y, zh, core = r // 4, (r // 2) % 2, r % 2

    def place(dx, dz):
        return ((x + dx + X) % X) * 2 + (z + dz) % 2

    def outer(dy, dz, dc):
        return (((y + dy + Y) % Y) * 2 + (zh + dz) % 2) * 2 + (core + dc) % 2

    right = {"fsdp": place(1, 0)}
    left = {"fsdp": place(-1, 0)}
    across = {"fsdp": place(0, 1)}
    twin = {"replica": outer(0, 0, 1)}
    ypeers = [{"replica": outer(d, 0, 0)} for d in (1, -1)]
    far = {"replica": outer(0, 1, 0)}

    barrier = pltpu.get_barrier_semaphore()
    peers = [right, left, across, twin, far] + ypeers
    for peer in peers:
        pl.semaphore_signal(barrier, inc=1, device_id=peer, device_id_type=MESH)

    def w_copy(c, side):
        return pltpu.make_async_copy(
            w_h.at[
                pl.ds(pl.multiple_of(c // groups * shard, 16), shard),
                pl.ds(pl.multiple_of((side * groups + c % groups) * HEAD, HEAD), HEAD),
            ],
            wbuf.at[c, pl.ds(pl.multiple_of(f * shard, 16), shard), pl.ds(side * HEAD, HEAD)],
            w_sem.at[c, side],
        )

    loads = [
        pltpu.make_async_copy(a, b, in_sem.at[i])
        for i, (a, b) in enumerate(
            ((loc_h, loc), (base_h, base), (tok_h, tok), (q_h, q), (mast_h, mast), (mom_h, mom))
        )
    ]
    for c in range(chunks):
        for side in range(2):
            w_copy(c, side).start()
    for load in loads:
        load.start()

    kinds = (
        (place(0, 0), half, half, across, place(0, 1)),
        (place(0, 0), 0, shard, right, place(-1, 0)),
        (place(0, 0), 0, shard, left, place(1, 0)),
        (place(0, 1), half, half, right, place(-1, 1)),
        (place(0, 1), half, half, left, place(1, 1)),
        (place(-1, 0), 0, half, right, place(2, 0)),
        (place(1, 0), half, half, left, place(2, 0)),
        (place(-1, 1), half, quarter, right, place(2, 1)),
        (place(1, 1), half + quarter, quarter, left, place(2, 1)),
    )

    def tok_copy(h, xx, arriving):
        cols = pl.ds(pl.multiple_of((xx * 2 + 1 - z) * whole + h * shard, half), half)
        there = theirs.at[:, pl.ds((h * X + xx) * half, half)]
        return pltpu.make_async_remote_copy(
            src_ref=there if arriving else tok.at[:, cols], dst_ref=there, send_sem=tok_send.at[h, xx],
            recv_sem=tok_recv.at[h, xx], device_id=across, device_id_type=MESH,
        )

    def sums_back(g):
        return pltpu.make_async_remote_copy(
            src_ref=given.at[g], dst_ref=gained.at[g], send_sem=g_send.at[g], recv_sem=g_recv.at[g],
            device_id=across, device_id_type=MESH,
        )

    def moved(k, g, arriving):
        source, start, count, target, other = kinds[k]
        held = other if arriving else source
        part = wbuf.at[g, pl.ds(pl.multiple_of(held * shard + start, 16), count), :]
        return pltpu.make_async_remote_copy(
            src_ref=part,
            dst_ref=part,
            send_sem=kv_send.at[g, k],
            recv_sem=kv_recv.at[g, k],
            device_id=target,
            device_id_type=MESH,
        )

    def send(g, *which):
        for k in which:
            moved(k, g, False).start()

    def arrived(g, *which):
        for k in which:
            moved(k, g, True).wait_recv()

    def own(g):
        w_copy(g, 0).wait()
        w_copy(g, 1).wait()
        send(g, 0, 1, 2)

    pl.semaphore_wait(barrier, len(peers))
    for c in range(LEAD):
        own(c)

    loads[2].wait()
    for xx in range(X):
        tok_copy(0, xx, False).start()
    given[...] = jnp.zeros_like(given)
    acc[...] = jnp.zeros_like(acc)

    ends = []
    total = len_s[0]
    for i in range(len_s.shape[0] - 1):
        ends.append(total)
        total = total + len_s[i + 1]
    row_at = lax.broadcasted_iota(jnp.int32, (tokens, 1), 0)
    col_at = lax.broadcasted_iota(jnp.int32, (1, tokens), 1)
    row_doc = jnp.zeros((tokens, 1), jnp.int32)
    col_doc = jnp.zeros((1, tokens), jnp.int32)
    for end in ends:
        row_doc += (row_at >= end).astype(jnp.int32)
        col_doc += (col_at >= end).astype(jnp.int32)
    allowed = jnp.logical_and(row_doc == col_doc, col_at <= row_at)
    bias[...] = jnp.where(allowed, 0.0, -1e30).astype(F32)

    tile = 32

    def decoded(row, col):
        grad = base[pl.ds(row, tile), pl.ds(col, BLK)].astype(F32) - loc[pl.ds(row, tile), pl.ds(col, BLK)].astype(F32)
        top = jnp.max(jnp.abs(grad), axis=1, keepdims=True)
        scale = ((top + 1e-6) / QUANT_RANGE).astype(BF).astype(F32)
        return (grad / scale).astype(BF).astype(F32) * scale

    def over_block(j, side, store):
        first = pl.multiple_of((2 * j + side) * owned, owned)

        def step(t, carry):
            row = pl.multiple_of(t * tile, tile)
            for b in range(owned // BLK):
                store(row, b * BLK, decoded(row, pl.multiple_of(first + b * BLK, BLK)))
            return carry

        lax.fori_loop(0, rows // tile, step, 0)

    def c_copy(j):
        return pltpu.make_async_remote_copy(
            src_ref=csend.at[j], dst_ref=crecv.at[j], send_sem=c_send.at[j], recv_sem=c_recv.at[j],
            device_id=twin, device_id_type=MESH,
        )

    def ahead(d):
        return (y + d + Y) % Y

    def y_half(way):
        return pltpu.make_async_remote_copy(
            src_ref=ysend.at[2 * ahead(2) + way], dst_ref=yhalf.at[way], send_sem=y_send.at[way],
            recv_sem=y_recv.at[way], device_id=ypeers[way], device_id_type=MESH,
        )

    def y_pair(way):
        return pltpu.make_async_remote_copy(
            src_ref=ysend.at[pl.ds(2 * ahead(1 - 2 * way), 2)], dst_ref=yrecv.at[way], send_sem=y_send.at[2 + way],
            recv_sem=y_recv.at[2 + way], device_id=ypeers[way], device_id_type=MESH,
        )

    def z_copy():
        return pltpu.make_async_remote_copy(
            src_ref=zsend, dst_ref=zrecv, send_sem=z_send, recv_sem=z_recv, device_id=far, device_id_type=MESH
        )

    def fz_copy(arriving):
        part = fbuf.at[core, 2 * y + (1 - zh if arriving else zh)]
        return pltpu.make_async_remote_copy(
            src_ref=part, dst_ref=part, send_sem=fz_send, recv_sem=fz_recv, device_id=far, device_id_type=MESH
        )

    def f_pair(way, arriving):
        part = fbuf.at[core, pl.ds(2 * (ahead(2 * way - 1) if arriving else y), 2)]
        return pltpu.make_async_remote_copy(
            src_ref=part, dst_ref=part, send_sem=fy_send.at[way], recv_sem=fy_recv.at[way],
            device_id=ypeers[way], device_id_type=MESH,
        )

    def f_half(way, arriving):
        part = fbuf.at[core, 2 * ahead(2 if arriving else 2 * way - 1) + way]
        return pltpu.make_async_remote_copy(
            src_ref=part, dst_ref=part, send_sem=fy_send.at[2 + way], recv_sem=fy_recv.at[2 + way],
            device_id=ypeers[way], device_id_type=MESH,
        )

    def fc_copy(d, arriving):
        at = pl.ds(2 * ahead(d), 2)
        part = fbuf.at[1 - core, at] if arriving else fbuf.at[core, at]
        return pltpu.make_async_remote_copy(
            src_ref=part, dst_ref=part, send_sem=fc_send.at[d + 1], recv_sem=fc_recv.at[d + 1],
            device_id=twin, device_id_type=MESH,
        )

    def f_out(side, j):
        return pltpu.make_async_copy(
            fbuf.at[side, j],
            fresh_o.at[:, pl.ds(pl.multiple_of((2 * j + side) * owned, owned), owned)],
            fo_sem.at[side, j],
        )

    loads[0].wait()
    loads[1].wait()

    def for_twin(j, carry):
        def store(row, col, value):
            csend[j, pl.ds(row, tile), pl.ds(col, BLK)] = value.astype(BF)

        over_block(j, 1 - core, store)
        c_copy(j).start()
        return carry

    lax.fori_loop(0, pairs, for_twin, 0)

    def with_twin(j, carry):
        c_copy(j).wait_recv()

        def store(row, col, value):
            at = (j, pl.ds(row, tile), pl.ds(col, BLK))
            ysend[at] = (value + crecv[at].astype(F32)).astype(BF)

        over_block(j, core, store)
        return carry

    def sum_y(part, row):
        at = pl.ds(row, tile)
        value = ysend[2 * y + part, at, :].astype(F32)
        for way in range(2):
            value = value + yrecv[way, part, at, :].astype(F32)
        return value

    def row_tiles(body):
        def step(t, carry):
            body(pl.multiple_of(t * tile, tile))
            return carry

        lax.fori_loop(0, rows // tile, step, 0)

    def product(tokens_of, first, c, row, count):
        return jnp.dot(
            tokens_of[:, pl.ds(pl.multiple_of(first, half), count)],
            wbuf[c, pl.ds(pl.multiple_of(row, half), count), :],
            preferred_element_type=F32,
        )

    def give(c):
        g, h = c % groups, c // groups
        for xx in range(X):
            given[g] += product(theirs, (h * X + xx) * half, c, (xx * 2 + z) * shard, half)

    def adder(c):
        g, h = c % groups, c // groups

        def add(held, start, count):
            acc[g] += product(tok, held * whole + h * shard + start, c, held * shard + start, count)

        return add

    def keep(c):
        add = adder(c)
        add(place(0, 0), 0, shard)
        add(place(-1, 0), 0, shard)
        add(place(1, 0), 0, shard)
        arrived(c, 6)
        add(place(2, 0), 0, shard)

    def compute(c):
        g, h = c % groups, c // groups
        add = adder(c)
        add(place(0, 1), half, half)
        add(place(-1, 1), half, half)
        add(place(1, 1), half, half)
        arrived(c, 7, 8)
        add(place(2, 1), half, half)

        @pl.when(h == PARTS - 1)
        def _():
            sums_back(g).wait_recv()
            packed[...] = (acc[g] + gained[g]).astype(BF)

            @pl.when(g < groups - 1)
            def _():
                first = pl.multiple_of(g * per_group * HEAD, HEAD)
                attend(q, first, packed, bias, att, first, per_group)


    def turn(t, carry):
        @pl.when(t < chunks)
        def _():
            arrived(t, 1)
            send(t, 5)
            arrived(t, 2)
            send(t, 6)

        @pl.when(t + LEAD < chunks)
        def _():
            own(t + LEAD)

        @pl.when(t == 1)
        def _():
            for xx in range(X // 2):
                tok_copy(1, xx, False).start()

        @pl.when(t == 2)
        def _():
            for xx in range(X // 2, X):
                tok_copy(1, xx, False).start()

        @pl.when(t == 1)
        def _():
            for xx in range(X):
                tok_copy(0, xx, True).wait_recv()

        @pl.when(t == groups + 1)
        def _():
            for xx in range(X):
                tok_copy(1, xx, True).wait_recv()

        @pl.when(jnp.logical_and(t > 1, t <= chunks + 1))
        def _():
            arrived(t - 2, 0)
            send(t - 2, 3, 4)

        @pl.when(jnp.logical_and(t > 0, t <= chunks))
        def _():
            arrived(t - 1, 5)
            give(t - 1)

        @pl.when(jnp.logical_and(t > groups, t <= chunks))
        def _():
            sums_back(t - 1 - groups).start()

        @pl.when(jnp.logical_and(t > 2, t <= chunks + 2))
        def _():
            arrived(t - 3, 3)
            send(t - 3, 7)
            arrived(t - 3, 4)
            send(t - 3, 8)

        @pl.when(jnp.logical_and(t > 0, t <= chunks))
        def _():
            keep(t - 1)

        @pl.when(t == 0)
        def _():
            lax.fori_loop(0, pairs, with_twin, 0)
            for way in range(2):
                y_half(way).start()
            for load in loads[3:]:
                load.wait()

        @pl.when(t == 1)
        def _():
            for way in range(2):
                y_half(way).wait_recv()
                onward = 2 * ahead(1 - 2 * way) + way

                def body(row):
                    at = pl.ds(row, tile)
                    value = ysend[onward, at, :].astype(F32) + yhalf[way, at, :].astype(F32)
                    ysend[onward, at, :] = value.astype(BF)

                row_tiles(body)
                y_pair(way).start()

        @pl.when(t == 2)
        def _():
            for way in range(2):
                y_pair(way).wait_recv()

            def body(row):
                zsend[pl.ds(row, tile), :] = sum_y(1 - zh, row).astype(BF)
                zown[pl.ds(row, tile), :] = sum_y(zh, row)

            row_tiles(body)
            z_copy().start()

        @pl.when(t == 4)
        def _():
            z_copy().wait_recv()

            def body(row):
                at = pl.ds(row, tile)
                averaged = (zown[at, :] + zrecv[at, :].astype(F32)) * (1.0 / 16)
                moved_on = MOMENTUM_COEF * mom[at, :] + averaged
                updated = mast[at, :] - OUTER_RATE * (averaged + MOMENTUM_COEF * moved_on)
                mom_o[at, :] = moved_on
                mast_o[at, :] = updated
                fbuf[core, 2 * y + zh, at, :] = updated.astype(BF)

            row_tiles(body)
            fz_copy(False).start()

        @pl.when(t == 6)
        def _():
            fz_copy(True).wait_recv()
            for way in range(2):
                f_pair(way, False).start()
            fc_copy(0, False).start()

        @pl.when(t == 7)
        def _():
            for way in range(2):
                f_pair(way, True).wait_recv()
                f_half(way, False).start()
                fc_copy(2 * way - 1, False).start()

        @pl.when(t == 8)
        def _():
            for way in range(2):
                f_half(way, True).wait_recv()
            fc_copy(2, False).start()

            def out_own(j, carry):
                f_out(core, j).start()
                return carry

            lax.fori_loop(0, pairs, out_own, 0)

        @pl.when(t == chunks + 2)
        def _():
            for d in range(-1, Y - 1):
                fc_copy(d, True).wait_recv()

            def out_twin(j, carry):
                f_out(1 - core, j).start()
                return carry

            lax.fori_loop(0, pairs, out_twin, 0)

        @pl.when(t > 3)
        def _():
            compute(t - 4)

        return carry

    lax.fori_loop(0, chunks + 4, turn, 0)

    def sent(g, carry):
        for k in range(len(kinds)):
            moved(k, g, False).wait_send()
        return carry

    lax.fori_loop(0, chunks, sent, 0)
    for h in range(PARTS):
        for xx in range(X):
            tok_copy(h, xx, False).wait_send()
    for g in range(groups):
        sums_back(g).wait_send()

    def c_sent(j, carry):
        c_copy(j).wait_send()
        f_out(0, j).wait()
        f_out(1, j).wait()
        return carry

    lax.fori_loop(0, pairs, c_sent, 0)
    for way in range(2):
        y_half(way).wait_send()
        y_pair(way).wait_send()
        f_pair(way, False).wait_send()
        f_half(way, False).wait_send()
    for d in range(-1, Y - 1):
        fc_copy(d, False).wait_send()
    z_copy().wait_send()
    fz_copy(False).wait_send()


def write_out(q_h, att, mast, mom, fresh, packed, bias, att_o, mast_o, mom_o, fresh_o, q, last, sem):
    done = att.shape[1]
    more = last.shape[1]
    load = pltpu.make_async_copy(q_h.at[:, pl.ds(done, more)], q, sem.at[0])
    load.start()
    pairs = ((att, att_o.at[:, pl.ds(0, done)]), (fresh, fresh_o), (mast, mast_o), (mom, mom_o))
    copies = [pltpu.make_async_copy(src, dst, sem.at[i + 1]) for i, (src, dst) in enumerate(pairs)]
    for copy in copies:
        copy.start()
    load.wait()
    attend(q, 0, packed, bias, last, 0, more // HEAD)
    copies.append(pltpu.make_async_copy(last, att_o.at[:, pl.ds(done, more)], sem.at[len(pairs) + 1]))
    copies[-1].start()
    for copy in copies:
        copy.wait()


def shards(tokens, queries, kv_weight, doc_lengths, local_params, base_copy, master, momentum):
    tok_count, width = tokens.shape[1:]
    q_width = queries.shape[2]
    shard, kv_width = kv_weight.shape[1:]
    rows, full = base_copy.shape
    owned = master.shape[1]
    groups = kv_width // (2 * HEAD)
    pairs = full // owned // 2
    hbm = pl.BlockSpec(memory_space=pl.ANY)
    dma = pltpu.SemaphoreType.DMA
    outs = pl.pallas_call(
        kernel,
        out_shape=(
            pltpu.VMEM((tok_count, q_width - q_width // groups), BF),
            pltpu.VMEM((rows, owned), F32),
            pltpu.VMEM((rows, owned), F32),
            pltpu.VMEM((rows, full), BF),
            pltpu.VMEM((tok_count, 2 * HEAD), BF),
            pltpu.VMEM((tok_count, tok_count), F32),
        ),
        in_specs=[hbm] * 3 + [pl.BlockSpec(memory_space=pltpu.SMEM)] + [hbm] * 4,
        out_specs=(pl.BlockSpec(memory_space=pltpu.VMEM),) * 6,
        scratch_shapes=[
            pltpu.VMEM((groups * PARTS, width // PARTS, 2 * HEAD), BF),
            pltpu.VMEM((tok_count, width), BF),
            pltpu.VMEM((tok_count, q_width), BF),
            pltpu.VMEM((rows, full), BF),
            pltpu.VMEM((rows, full), BF),
            pltpu.VMEM((pairs, rows, owned), BF),
            pltpu.VMEM((pairs, rows, owned), BF),
            pltpu.VMEM((pairs, rows, owned), BF),
            pltpu.VMEM((2, rows, owned), BF),
            pltpu.VMEM((2, 2, rows, owned), BF),
            pltpu.VMEM((rows, owned), BF),
            pltpu.VMEM((rows, owned), BF),
            pltpu.VMEM((rows, owned), F32),
            pltpu.VMEM((rows, owned), F32),
            pltpu.VMEM((rows, owned), F32),
            pltpu.VMEM((2, pairs, rows, owned), BF),
            pltpu.VMEM((groups, tok_count, 2 * HEAD), F32),
            pltpu.VMEM((groups, tok_count, 2 * HEAD), F32),
            pltpu.VMEM((groups, tok_count, 2 * HEAD), F32),
            pltpu.VMEM((tok_count, width // 4), BF),
            dma((groups * PARTS, 9)),
            dma((groups * PARTS, 9)),
            dma((PARTS, X)),
            dma((PARTS, X)),
            dma((groups,)),
            dma((groups,)),
            dma((pairs,)),
            dma((pairs,)),
            dma((4,)),
            dma((4,)),
            dma,
            dma,
            dma,
            dma,
            dma((4,)),
            dma((4,)),
            dma((Y,)),
            dma((Y,)),
            dma((groups * PARTS, 2)),
            dma((6,)),
            dma((2, pairs)),
        ],
        compiler_params=pltpu.CompilerParams(
            collective_id=0, has_side_effects=True, vmem_limit_bytes=51 * 1024 * 1024
        ),
        cost_estimate=pl.CostEstimate(flops=9 * 10**9, bytes_accessed=3 * 10**7, transcendentals=5 * 10**6),
        name="fused",
    )(
        tokens[0], queries[0], kv_weight[0], doc_lengths[0, 0], local_params[0], base_copy, master, momentum
    )
    attended, new_master, new_momentum, fresh = pl.pallas_call(
        write_out,
        out_shape=(
            jax.ShapeDtypeStruct((tok_count, q_width), BF),
            jax.ShapeDtypeStruct((rows, owned), F32),
            jax.ShapeDtypeStruct((rows, owned), F32),
            jax.ShapeDtypeStruct((rows, full), BF),
        ),
        in_specs=[hbm] + [pl.BlockSpec(memory_space=pltpu.VMEM)] * 6,
        out_specs=(hbm,) * 4,
        scratch_shapes=[
            pltpu.VMEM((tok_count, q_width // groups), BF),
            pltpu.VMEM((tok_count, q_width // groups), BF),
            dma((6,)),
        ],
        compiler_params=pltpu.CompilerParams(vmem_limit_bytes=12 * 1024 * 1024),
        name="write_out",
    )(queries[0], *outs)
    return attended[None], new_master, new_momentum, fresh


def solution(mesh):
    return jax.shard_map(
        shards,
        mesh=mesh,
        in_specs=(
            P("replica", "fsdp", None),
            P("replica", "fsdp", None),
            P("replica", "fsdp", None),
            P("replica", "fsdp", None),
            P("replica", "fsdp", None),
            P("fsdp", None),
            P("fsdp", "replica"),
            P("fsdp", "replica"),
        ),
        out_specs=(P("replica", "fsdp", None), P("fsdp", "replica"), P("fsdp", "replica"), P("fsdp", None)),
        check_vma=False,
    )
```

```python
import jax
import jax.numpy as jnp
from jax import lax
from jax.experimental import pallas as pl
from jax.experimental.pallas import tpu as pltpu
from jax.sharding import PartitionSpec as P

MESH = pl.DeviceIdType.MESH
HEAD = 128
BLK = 128
MOMENTUM_COEF = 0.9
OUTER_RATE = 0.7
QUANT_RANGE = 448.0
LOG2E = 1.4426950408889634

X = 4
Y = 4
LEAD = 2
PARTS = 2
LATE = 16
BF = jnp.bfloat16
F32 = jnp.float32


def attend(q, q_first, packed, bias, att, att_first, heads):
    tokens = q.shape[0]
    nq = 3
    qrows = tokens // nq
    from_cols = [pl.ds(pl.multiple_of(q_first + h * HEAD, HEAD), HEAD) for h in range(heads)]
    to_cols = [pl.ds(pl.multiple_of(att_first + h * HEAD, HEAD), HEAD) for h in range(heads)]
    for i in range(nq):
        at = pl.ds(i * qrows, qrows)
        seen = (i + 1) * qrows
        scores = [
            lax.dot_general(q[at, cols], packed[:seen, :HEAD], (((1,), (1,)), ((), ())), preferred_element_type=F32)
            * (HEAD**-0.5 * LOG2E)
            + bias[at, :seen]
            for cols in from_cols
        ]
        highest = [jnp.max(s, axis=1, keepdims=True) for s in scores]
        expo = [jnp.exp2(s - m) for s, m in zip(scores, highest)]
        over = [1.0 / jnp.sum(e, axis=1, keepdims=True) for e in expo]
        for cols, e, o in zip(to_cols, expo, over):
            weights = (e * o).astype(BF)
            att[at, cols] = jnp.dot(weights, packed[:seen, HEAD:], preferred_element_type=F32).astype(BF)


def kernel(
    tok_h, q_h, w_h, len_s, loc_h, base_h, mast_h, mom_h,
    att, mast_o, mom_o, fresh_o, packed, bias,
    wbuf, tok, q, loc, base, csend, crecv, ysend, yhalf, yrecv, zsend, zrecv, zown, mast, mom, fbuf, acc, given, gained, theirs,
    kv_send, kv_recv, tok_send, tok_recv, g_send, g_recv, c_send, c_recv, y_send, y_recv, z_send, z_recv, fz_send, fz_recv, fy_send, fy_recv,
    fc_send, fc_recv, w_sem, in_sem, fo_sem,
):
    chunks = wbuf.shape[0]
    groups = chunks // PARTS
    tokens = tok.shape[0]
    whole = w_h.shape[0]
    shard = whole // PARTS
    rows, owned = mast.shape
    pairs = csend.shape[0]
    per_group = q.shape[1] // HEAD // groups
    half = shard // 2
    up = ((half - LATE) // 2 + 15) // 16 * 16

    f = lax.axis_index("fsdp")
    r = lax.axis_index("replica")
    x, z = f // 2, f % 2
    y, zh, core = r // 4, (r // 2) % 2, r % 2

    def place(dx, dz):
        return ((x + dx + X) % X) * 2 + (z + dz) % 2

    def outer(dy, dz, dc):
        return (((y + dy + Y) % Y) * 2 + (zh + dz) % 2) * 2 + (core + dc) % 2

    right = {"fsdp": place(1, 0)}
    left = {"fsdp": place(-1, 0)}
    across = {"fsdp": place(0, 1)}
    twin = {"replica": outer(0, 0, 1)}
    ypeers = [{"replica": outer(d, 0, 0)} for d in (1, -1)]
    far = {"replica": outer(0, 1, 0)}

    barrier = pltpu.get_barrier_semaphore()
    peers = [right, left, across, twin, far] + ypeers
    for peer in peers:
        pl.semaphore_signal(barrier, inc=1, device_id=peer, device_id_type=MESH)

    def w_copy(c, side):
        return pltpu.make_async_copy(
            w_h.at[
                pl.ds(pl.multiple_of(c // groups * shard, 16), shard),
                pl.ds(pl.multiple_of((side * groups + c % groups) * HEAD, HEAD), HEAD),
            ],
            wbuf.at[c, pl.ds(pl.multiple_of(f * shard, 16), shard), pl.ds(side * HEAD, HEAD)],
            w_sem.at[c, side],
        )

    loads = [
        pltpu.make_async_copy(a, b, in_sem.at[i])
        for i, (a, b) in enumerate(
            ((loc_h, loc), (base_h, base), (tok_h, tok), (q_h, q), (mast_h, mast), (mom_h, mom))
        )
    ]
    for c in range(chunks):
        for side in range(2):
            w_copy(c, side).start()
    for load in loads:
        load.start()

    kinds = (
        (place(0, 0), half, half, across, place(0, 1)),
        (place(0, 0), 0, shard, right, place(-1, 0)),
        (place(0, 0), 0, shard, left, place(1, 0)),
        (place(0, 1), half + LATE, half - LATE, right, place(-1, 1)),
        (place(0, 1), half + LATE, half - LATE, left, place(1, 1)),
        (place(-1, 0), 0, half, right, place(2, 0)),
        (place(1, 0), half, half, left, place(2, 0)),
        (place(-1, 1), half + LATE, up, right, place(2, 1)),
        (place(1, 1), half + LATE + up, half - LATE - up, left, place(2, 1)),
        (place(-1, 0), half, LATE, across, place(-1, 1)),
        (place(1, 0), half, LATE, across, place(1, 1)),
        (place(2, 0), half, LATE, across, place(2, 1)),
    )

    def tok_copy(h, xx, arriving):
        cols = pl.ds(pl.multiple_of((xx * 2 + 1 - z) * whole + h * shard, half), half)
        there = theirs.at[:, pl.ds((h * X + xx) * half, half)]
        return pltpu.make_async_remote_copy(
            src_ref=there if arriving else tok.at[:, cols], dst_ref=there, send_sem=tok_send.at[h, xx],
            recv_sem=tok_recv.at[h, xx], device_id=across, device_id_type=MESH,
        )

    def sums_back(g):
        return pltpu.make_async_remote_copy(
            src_ref=given.at[g], dst_ref=gained.at[g], send_sem=g_send.at[g], recv_sem=g_recv.at[g],
            device_id=across, device_id_type=MESH,
        )

    def moved(k, g, arriving):
        source, start, count, target, other = kinds[k]
        held = other if arriving else source
        part = wbuf.at[g, pl.ds(pl.multiple_of(held * shard + start, 16), count), :]
        return pltpu.make_async_remote_copy(
            src_ref=part,
            dst_ref=part,
            send_sem=kv_send.at[g, k],
            recv_sem=kv_recv.at[g, k],
            device_id=target,
            device_id_type=MESH,
        )

    def send(g, *which):
        for k in which:
            moved(k, g, False).start()

    def arrived(g, *which):
        for k in which:
            moved(k, g, True).wait_recv()

    def own(g):
        w_copy(g, 0).wait()
        w_copy(g, 1).wait()
        send(g, 0, 1, 2)

    pl.semaphore_wait(barrier, len(peers))
    for c in range(LEAD):
        own(c)

    loads[2].wait()
    for xx in range(X):
        tok_copy(0, xx, False).start()
    given[...] = jnp.zeros_like(given)
    acc[...] = jnp.zeros_like(acc)

    ends = []
    total = len_s[0]
    for i in range(len_s.shape[0] - 1):
        ends.append(total)
        total = total + len_s[i + 1]
    row_at = lax.broadcasted_iota(jnp.int32, (tokens, 1), 0)
    col_at = lax.broadcasted_iota(jnp.int32, (1, tokens), 1)
    row_doc = jnp.zeros((tokens, 1), jnp.int32)
    col_doc = jnp.zeros((1, tokens), jnp.int32)
    for end in ends:
        row_doc += (row_at >= end).astype(jnp.int32)
        col_doc += (col_at >= end).astype(jnp.int32)
    allowed = jnp.logical_and(row_doc == col_doc, col_at <= row_at)
    bias[...] = jnp.where(allowed, 0.0, -1e30).astype(F32)

    tile = 32

    def decoded(row, col):
        grad = base[pl.ds(row, tile), pl.ds(col, BLK)].astype(F32) - loc[pl.ds(row, tile), pl.ds(col, BLK)].astype(F32)
        top = jnp.max(jnp.abs(grad), axis=1, keepdims=True)
        scale = ((top + 1e-6) / QUANT_RANGE).astype(BF).astype(F32)
        return (grad / scale).astype(BF).astype(F32) * scale

    def over_block(j, side, store):
        first = pl.multiple_of((2 * j + side) * owned, owned)

        def step(t, carry):
            row = pl.multiple_of(t * tile, tile)
            for b in range(owned // BLK):
                store(row, b * BLK, decoded(row, pl.multiple_of(first + b * BLK, BLK)))
            return carry

        lax.fori_loop(0, rows // tile, step, 0)

    def c_copy(j):
        return pltpu.make_async_remote_copy(
            src_ref=csend.at[j], dst_ref=crecv.at[j], send_sem=c_send.at[j], recv_sem=c_recv.at[j],
            device_id=twin, device_id_type=MESH,
        )

    def ahead(d):
        return (y + d + Y) % Y

    def y_half(way):
        return pltpu.make_async_remote_copy(
            src_ref=ysend.at[2 * ahead(2) + way], dst_ref=yhalf.at[way], send_sem=y_send.at[way],
            recv_sem=y_recv.at[way], device_id=ypeers[way], device_id_type=MESH,
        )

    def y_pair(way):
        return pltpu.make_async_remote_copy(
            src_ref=ysend.at[pl.ds(2 * ahead(1 - 2 * way), 2)], dst_ref=yrecv.at[way], send_sem=y_send.at[2 + way],
            recv_sem=y_recv.at[2 + way], device_id=ypeers[way], device_id_type=MESH,
        )

    def z_copy():
        return pltpu.make_async_remote_copy(
            src_ref=zsend, dst_ref=zrecv, send_sem=z_send, recv_sem=z_recv, device_id=far, device_id_type=MESH
        )

    def fz_copy(arriving):
        part = fbuf.at[core, 2 * y + (1 - zh if arriving else zh)]
        return pltpu.make_async_remote_copy(
            src_ref=part, dst_ref=part, send_sem=fz_send, recv_sem=fz_recv, device_id=far, device_id_type=MESH
        )

    def f_pair(way, arriving):
        part = fbuf.at[core, pl.ds(2 * (ahead(2 * way - 1) if arriving else y), 2)]
        return pltpu.make_async_remote_copy(
            src_ref=part, dst_ref=part, send_sem=fy_send.at[way], recv_sem=fy_recv.at[way],
            device_id=ypeers[way], device_id_type=MESH,
        )

    def f_half(way, arriving):
        part = fbuf.at[core, 2 * ahead(2 if arriving else 2 * way - 1) + way]
        return pltpu.make_async_remote_copy(
            src_ref=part, dst_ref=part, send_sem=fy_send.at[2 + way], recv_sem=fy_recv.at[2 + way],
            device_id=ypeers[way], device_id_type=MESH,
        )

    def fc_copy(d, arriving):
        at = pl.ds(2 * ahead(d), 2)
        part = fbuf.at[1 - core, at] if arriving else fbuf.at[core, at]
        return pltpu.make_async_remote_copy(
            src_ref=part, dst_ref=part, send_sem=fc_send.at[d + 1], recv_sem=fc_recv.at[d + 1],
            device_id=twin, device_id_type=MESH,
        )

    def f_out(side, j):
        return pltpu.make_async_copy(
            fbuf.at[side, j],
            fresh_o.at[:, pl.ds(pl.multiple_of((2 * j + side) * owned, owned), owned)],
            fo_sem.at[side, j],
        )

    loads[0].wait()
    loads[1].wait()

    def for_twin(j, carry):
        def store(row, col, value):
            csend[j, pl.ds(row, tile), pl.ds(col, BLK)] = value.astype(BF)

        over_block(j, 1 - core, store)
        c_copy(j).start()
        return carry

    lax.fori_loop(0, pairs, for_twin, 0)

    def with_twin(j, carry):
        c_copy(j).wait_recv()

        def store(row, col, value):
            at = (j, pl.ds(row, tile), pl.ds(col, BLK))
            ysend[at] = (value + crecv[at].astype(F32)).astype(BF)

        over_block(j, core, store)
        return carry

    def sum_y(part, row):
        at = pl.ds(row, tile)
        value = ysend[2 * y + part, at, :].astype(F32)
        for way in range(2):
            value = value + yrecv[way, part, at, :].astype(F32)
        return value

    def row_tiles(body):
        def step(t, carry):
            body(pl.multiple_of(t * tile, tile))
            return carry

        lax.fori_loop(0, rows // tile, step, 0)

    def product(tokens_of, first, c, row, count):
        return jnp.dot(
            tokens_of[:, pl.ds(pl.multiple_of(first, half), count)],
            wbuf[c, pl.ds(pl.multiple_of(row, half), count), :],
            preferred_element_type=F32,
        )

    def give(c):
        g, h = c % groups, c // groups
        for xx in range(X):
            given[g] += product(theirs, (h * X + xx) * half, c, (xx * 2 + z) * shard, half)

    def adder(c):
        g, h = c % groups, c // groups

        def add(held, start, count):
            acc[g] += product(tok, held * whole + h * shard + start, c, held * shard + start, count)

        return add

    def keep(c):
        add = adder(c)
        add(place(0, 0), 0, shard)
        add(place(-1, 0), 0, shard)
        add(place(1, 0), 0, shard)
        arrived(c, 6)
        send(c, 11)
        add(place(2, 0), 0, shard)

    def compute(c):
        g, h = c % groups, c // groups
        add = adder(c)
        add(place(0, 1), half, half)
        arrived(c, 9, 10)
        add(place(-1, 1), half, half)
        add(place(1, 1), half, half)
        arrived(c, 7, 8, 11)
        add(place(2, 1), half, half)

        @pl.when(h == PARTS - 1)
        def _():
            sums_back(g).wait_recv()
            packed[...] = (acc[g] + gained[g]).astype(BF)

            @pl.when(g < groups - 1)
            def _():
                first = pl.multiple_of(g * per_group * HEAD, HEAD)
                attend(q, first, packed, bias, att, first, per_group)


    def turn(t, carry):
        @pl.when(t < chunks)
        def _():
            arrived(t, 1)
            send(t, 5, 9)
            arrived(t, 2)
            send(t, 6, 10)

        @pl.when(t + LEAD < chunks)
        def _():
            own(t + LEAD)

        @pl.when(t == 1)
        def _():
            for xx in range(X // 2):
                tok_copy(1, xx, False).start()

        @pl.when(t == 2)
        def _():
            for xx in range(X // 2, X):
                tok_copy(1, xx, False).start()

        @pl.when(t == 1)
        def _():
            for xx in range(X):
                tok_copy(0, xx, True).wait_recv()

        @pl.when(t == groups + 1)
        def _():
            for xx in range(X):
                tok_copy(1, xx, True).wait_recv()

        @pl.when(jnp.logical_and(t > 1, t <= chunks + 1))
        def _():
            arrived(t - 2, 0)
            send(t - 2, 3, 4)

        @pl.when(jnp.logical_and(t > 0, t <= chunks))
        def _():
            arrived(t - 1, 5)
            give(t - 1)

        @pl.when(jnp.logical_and(t > groups, t <= chunks))
        def _():
            sums_back(t - 1 - groups).start()

        @pl.when(jnp.logical_and(t > 2, t <= chunks + 2))
        def _():
            arrived(t - 3, 3)
            send(t - 3, 7)
            arrived(t - 3, 4)
            send(t - 3, 8)

        @pl.when(jnp.logical_and(t > 0, t <= chunks))
        def _():
            keep(t - 1)

        @pl.when(t == 0)
        def _():
            lax.fori_loop(0, pairs, with_twin, 0)
            for way in range(2):
                y_half(way).start()
            for load in loads[3:]:
                load.wait()

        @pl.when(t == 1)
        def _():
            for way in range(2):
                y_half(way).wait_recv()
                onward = 2 * ahead(1 - 2 * way) + way

                def body(row):
                    at = pl.ds(row, tile)
                    value = ysend[onward, at, :].astype(F32) + yhalf[way, at, :].astype(F32)
                    ysend[onward, at, :] = value.astype(BF)

                row_tiles(body)
                y_pair(way).start()

        @pl.when(t == 2)
        def _():
            for way in range(2):
                y_pair(way).wait_recv()

            def body(row):
                zsend[pl.ds(row, tile), :] = sum_y(1 - zh, row).astype(BF)
                zown[pl.ds(row, tile), :] = sum_y(zh, row)

            row_tiles(body)
            z_copy().start()

        @pl.when(t == 4)
        def _():
            z_copy().wait_recv()

            def body(row):
                at = pl.ds(row, tile)
                averaged = (zown[at, :] + zrecv[at, :].astype(F32)) * (1.0 / 16)
                moved_on = MOMENTUM_COEF * mom[at, :] + averaged
                updated = mast[at, :] - OUTER_RATE * (averaged + MOMENTUM_COEF * moved_on)
                mom_o[at, :] = moved_on
                mast_o[at, :] = updated
                fbuf[core, 2 * y + zh, at, :] = updated.astype(BF)

            row_tiles(body)
            fz_copy(False).start()

        @pl.when(t == 6)
        def _():
            fz_copy(True).wait_recv()
            for way in range(2):
                f_pair(way, False).start()
            fc_copy(0, False).start()

        @pl.when(t == 7)
        def _():
            for way in range(2):
                f_pair(way, True).wait_recv()
                f_half(way, False).start()
                fc_copy(2 * way - 1, False).start()

        @pl.when(t == 8)
        def _():
            for way in range(2):
                f_half(way, True).wait_recv()
            fc_copy(2, False).start()

            def out_own(j, carry):
                f_out(core, j).start()
                return carry

            lax.fori_loop(0, pairs, out_own, 0)

        @pl.when(t == chunks + 2)
        def _():
            for d in range(-1, Y - 1):
                fc_copy(d, True).wait_recv()

            def out_twin(j, carry):
                f_out(1 - core, j).start()
                return carry

            lax.fori_loop(0, pairs, out_twin, 0)

        @pl.when(t > 4)
        def _():
            for k in range(len(kinds)):
                moved(k, t - 5, False).wait_send()

        @pl.when(t == chunks + 1)
        def _():
            def c_sent(j, carry):
                c_copy(j).wait_send()
                return carry

            lax.fori_loop(0, pairs, c_sent, 0)
            for way in range(2):
                y_half(way).wait_send()
                y_pair(way).wait_send()
                f_pair(way, False).wait_send()
                f_half(way, False).wait_send()
            for d in range(-1, Y - 1):
                fc_copy(d, False).wait_send()
            z_copy().wait_send()
            fz_copy(False).wait_send()
            for h in range(PARTS):
                for xx in range(X):
                    tok_copy(h, xx, False).wait_send()
            for g in range(groups - 1):
                sums_back(g).wait_send()

        @pl.when(t == chunks + 3)
        def _():
            def written(j, carry):
                f_out(0, j).wait()
                f_out(1, j).wait()
                return carry

            lax.fori_loop(0, pairs, written, 0)

        @pl.when(t > 3)
        def _():
            compute(t - 4)

        return carry

    lax.fori_loop(0, chunks + 4, turn, 0)

    for k in range(len(kinds)):
        moved(k, chunks - 1, False).wait_send()
    sums_back(groups - 1).wait_send()


def write_out(q_h, att, mast, mom, fresh, packed, bias, att_o, mast_o, mom_o, fresh_o, q, last, sem):
    done = att.shape[1]
    more = last.shape[1]
    load = pltpu.make_async_copy(q_h.at[:, pl.ds(done, more)], q, sem.at[0])
    load.start()
    pairs = ((att, att_o.at[:, pl.ds(0, done)]), (fresh, fresh_o), (mast, mast_o), (mom, mom_o))
    copies = [pltpu.make_async_copy(src, dst, sem.at[i + 1]) for i, (src, dst) in enumerate(pairs)]
    for copy in copies:
        copy.start()
    load.wait()
    attend(q, 0, packed, bias, last, 0, more // HEAD)
    copies.append(pltpu.make_async_copy(last, att_o.at[:, pl.ds(done, more)], sem.at[len(pairs) + 1]))
    copies[-1].start()
    for copy in copies:
        copy.wait()


def shards(tokens, queries, kv_weight, doc_lengths, local_params, base_copy, master, momentum):
    tok_count, width = tokens.shape[1:]
    q_width = queries.shape[2]
    shard, kv_width = kv_weight.shape[1:]
    rows, full = base_copy.shape
    owned = master.shape[1]
    groups = kv_width // (2 * HEAD)
    pairs = full // owned // 2
    hbm = pl.BlockSpec(memory_space=pl.ANY)
    dma = pltpu.SemaphoreType.DMA
    outs = pl.pallas_call(
        kernel,
        out_shape=(
            pltpu.VMEM((tok_count, q_width - q_width // groups), BF),
            pltpu.VMEM((rows, owned), F32),
            pltpu.VMEM((rows, owned), F32),
            pltpu.VMEM((rows, full), BF),
            pltpu.VMEM((tok_count, 2 * HEAD), BF),
            pltpu.VMEM((tok_count, tok_count), F32),
        ),
        in_specs=[hbm] * 3 + [pl.BlockSpec(memory_space=pltpu.SMEM)] + [hbm] * 4,
        out_specs=(pl.BlockSpec(memory_space=pltpu.VMEM),) * 6,
        scratch_shapes=[
            pltpu.VMEM((groups * PARTS, width // PARTS, 2 * HEAD), BF),
            pltpu.VMEM((tok_count, width), BF),
            pltpu.VMEM((tok_count, q_width), BF),
            pltpu.VMEM((rows, full), BF),
            pltpu.VMEM((rows, full), BF),
            pltpu.VMEM((pairs, rows, owned), BF),
            pltpu.VMEM((pairs, rows, owned), BF),
            pltpu.VMEM((pairs, rows, owned), BF),
            pltpu.VMEM((2, rows, owned), BF),
            pltpu.VMEM((2, 2, rows, owned), BF),
            pltpu.VMEM((rows, owned), BF),
            pltpu.VMEM((rows, owned), BF),
            pltpu.VMEM((rows, owned), F32),
            pltpu.VMEM((rows, owned), F32),
            pltpu.VMEM((rows, owned), F32),
            pltpu.VMEM((2, pairs, rows, owned), BF),
            pltpu.VMEM((groups, tok_count, 2 * HEAD), F32),
            pltpu.VMEM((groups, tok_count, 2 * HEAD), F32),
            pltpu.VMEM((groups, tok_count, 2 * HEAD), F32),
            pltpu.VMEM((tok_count, width // 4), BF),
            dma((groups * PARTS, 12)),
            dma((groups * PARTS, 12)),
            dma((PARTS, X)),
            dma((PARTS, X)),
            dma((groups,)),
            dma((groups,)),
            dma((pairs,)),
            dma((pairs,)),
            dma((4,)),
            dma((4,)),
            dma,
            dma,
            dma,
            dma,
            dma((4,)),
            dma((4,)),
            dma((Y,)),
            dma((Y,)),
            dma((groups * PARTS, 2)),
            dma((6,)),
            dma((2, pairs)),
        ],
        compiler_params=pltpu.CompilerParams(
            collective_id=0, has_side_effects=True, vmem_limit_bytes=51 * 1024 * 1024
        ),
        cost_estimate=pl.CostEstimate(flops=9 * 10**9, bytes_accessed=3 * 10**7, transcendentals=5 * 10**6),
        name="fused",
    )(
        tokens[0], queries[0], kv_weight[0], doc_lengths[0, 0], local_params[0], base_copy, master, momentum
    )
    attended, new_master, new_momentum, fresh = pl.pallas_call(
        write_out,
        out_shape=(
            jax.ShapeDtypeStruct((tok_count, q_width), BF),
            jax.ShapeDtypeStruct((rows, owned), F32),
            jax.ShapeDtypeStruct((rows, owned), F32),
            jax.ShapeDtypeStruct((rows, full), BF),
        ),
        in_specs=[hbm] + [pl.BlockSpec(memory_space=pltpu.VMEM)] * 6,
        out_specs=(hbm,) * 4,
        scratch_shapes=[
            pltpu.VMEM((tok_count, q_width // groups), BF),
            pltpu.VMEM((tok_count, q_width // groups), BF),
            dma((6,)),
        ],
        compiler_params=pltpu.CompilerParams(vmem_limit_bytes=12 * 1024 * 1024),
        name="write_out",
    )(queries[0], *outs)
    return attended[None], new_master, new_momentum, fresh


def solution(mesh):
    return jax.shard_map(
        shards,
        mesh=mesh,
        in_specs=(
            P("replica", "fsdp", None),
            P("replica", "fsdp", None),
            P("replica", "fsdp", None),
            P("replica", "fsdp", None),
            P("replica", "fsdp", None),
            P("fsdp", None),
            P("fsdp", "replica"),
            P("fsdp", "replica"),
        ),
        out_specs=(P("replica", "fsdp", None), P("fsdp", "replica"), P("fsdp", "replica"), P("fsdp", None)),
        check_vma=False,
    )
```
